32 devices in a mesh: wide: 4 (over x, core), narrow: 8 (over z, y).
Axes of the slice: x: 2, y: 2, z: 4, core: 2. Of those that a mesh axis runs over, the one named last changes fastest.
Arguments:
- node_feats: bfloat16 [28672, 256], P('narrow'), may hold values from -6 to 6
- grad_out: bfloat16 [28672, 256], P('narrow'), may hold values from -6 to 6
- tile_weight: bfloat16 [4, 8, 32, 128, 128], P('wide', 'narrow'), may hold values from -0.25 to 0.25
- tile_row: int32 [4, 8, 32], P('wide', 'narrow'), may hold values from 0 to 27
- src_block: int32 [4, 8, 32], P('wide', 'narrow'), may hold values from 0 to 27, as said below
- tile_count: int32 [4, 8, 8], P('wide', 'narrow'), may hold values from 1 to 4, as said below
- w_self: bfloat16 [256, 256], replicated, may hold values from -0.375 to 0.375
- w_out: bfloat16 [256, 256], replicated, may hold values from -0.375 to 0.375
- w_in: bfloat16 [256, 256], replicated, may hold values from -0.375 to 0.375
Outputs:
- hidden: bfloat16 [28672, 256], P('narrow')
- grad_feats: bfloat16 [28672, 256], P('narrow')
- grad_w_self: float32 [256, 256], replicated
- grad_w_out: float32 [256, 256], replicated
- grad_w_in: float32 [256, 256], replicated
The draws below stay inside these ranges and needn't reach their ends.
Inputs may be any that keep to these rules, and one draw needn't show every extreme that they name: `src_block`: on each device the 4 slots of one owner name different blocks. `tile_count`: the live slots of an owner are its first ones.
All inputs are finite; a program needn't handle non-finite values.
Results may differ from the reference program's by a relative error of at most 0.0057.
Values may be sent and summed in bfloat16 or wider, within the bound.
No kernel may reach another device: no remote copies, remote signals or barrier semaphores. Data moves between devices by JAX's collectives and lax.ppermute only.
A program may use at most 128 MiB of HBM per device.

```python
import jax
import jax.numpy as jnp
from jax import lax

D = 256
BS = 128
CAP = 4
BPN = 28
TILES_DEV = 32
NODES = 28672
N_WIDE = 4
N_NARROW = 8


def draw_src_block(key, part):
    scores = jax.random.randint(jax.random.fold_in(key, 11), (N_WIDE, N_NARROW, N_NARROW, BPN), 0, 1 << 20)
    scores = scores * BPN + jnp.arange(BPN, dtype=jnp.int32)
    order = jnp.argsort(scores, axis=-1)
    return order[..., :CAP].reshape(N_WIDE, N_NARROW, N_NARROW * CAP).astype(jnp.int32)


def draw_tile_count(key, part):
    base = jax.random.randint(jax.random.fold_in(key, 21), (N_WIDE, N_NARROW, N_NARROW), 1, CAP + 1)
    own_full = jax.random.randint(jax.random.fold_in(key, 22), (N_WIDE, N_NARROW, 1), 0, N_NARROW)
    dev_full = jax.random.randint(jax.random.fold_in(key, 23), (N_WIDE, 1, 1), 0, N_NARROW)
    col_full = jax.random.randint(jax.random.fold_in(key, 24), (N_WIDE, 1, 1), 0, N_NARROW)
    owner_ids = jnp.arange(N_NARROW, dtype=jnp.int32)
    full = (owner_ids[None, None, :] == own_full) | (owner_ids[None, :, None] == dev_full) | (owner_ids[None, None, :] == col_full)
    return jnp.where(full, CAP, base).astype(jnp.int32)


def touch_ends(result, rng, smallest, high):
    longest = result.shape.index(max(result.shape))
    spots = []
    for shift in (0, 1):
        where = [jax.random.randint(jax.random.fold_in(rng, axis), (), 0, length) for axis, length in enumerate(result.shape)]
        where[longest] = (where[longest] + shift) % result.shape[longest]
        spots.append(tuple(where))
    return result.at[spots[0]].set(smallest).at[spots[1]].set(high)


def steps_of(key, extent, cuts, low, high):
    def one(axis_at, parts):
        heights = jax.random.uniform(jax.random.fold_in(jax.random.fold_in(key, 6), axis_at), (parts,), jnp.float32, low / len(cuts), high / len(cuts))
        return jnp.repeat(jnp.exp(heights), extent[axis_at] // parts).reshape((-1,) + (1,) * (len(extent) - axis_at - 1))

    gain = one(*cuts[0])
    for cut in cuts[1:]:
        gain = gain * one(*cut)
    return gain


def bell_draw(key, shape, width, most, split=(), kind=jnp.bfloat16):
    drawn = jax.random.normal(key, shape, jnp.float32) * width
    if len(split) > 0:
        drawn = steps_of(key, shape, split, -0.22, 0.18) * drawn
    return jnp.clip(drawn, min=-most, max=most).astype(kind)


def setup_inputs(seed: int = 0) -> dict:
    keys = jax.random.split(jax.random.key(seed), 10)
    node_feats = bell_draw(keys[0], (NODES, D), 1.0, 6.0, ((0, 8),))
    grad_out = bell_draw(keys[1], (NODES, D), 1.0, 6.0, ((0, 8),))
    tile_weight = bell_draw(keys[2], (N_WIDE, N_NARROW, TILES_DEV, BS, BS), (N_WIDE * TILES_DEV * BS // BPN) ** -0.5, 0.25, ((0, 4), (1, 8)))
    tile_row = touch_ends(jax.random.randint(keys[3], (N_WIDE, N_NARROW, TILES_DEV), 0, BPN), jax.random.fold_in(keys[3], 1), 0, BPN - 1).astype(jnp.int32)
    src_block = draw_src_block(jax.random.fold_in(keys[9], 71), 0)
    tile_count = draw_tile_count(jax.random.fold_in(keys[9], 71), 0)
    w_self = bell_draw(keys[6], (D, D), D ** -0.5, 0.375)
    w_out = bell_draw(keys[7], (D, D), D ** -0.5, 0.375)
    w_in = bell_draw(keys[8], (D, D), D ** -0.5, 0.375)
    return dict(node_feats=node_feats, grad_out=grad_out, tile_weight=tile_weight, tile_row=tile_row, src_block=src_block, tile_count=tile_count, w_self=w_self, w_out=w_out, w_in=w_in)


def spread(forward_src, back_src, tiles, rows_glob, cols_glob, live):
    blocks = BPN * N_NARROW
    fwd_blocks = forward_src.reshape(blocks, BS, D).astype(jnp.float32)
    back_blocks = back_src.reshape(blocks, BS, D).astype(jnp.float32)

    def step(carry, item):
        acc_ahead, acc_back = carry
        tile_set, row_ids, col_ids, live_set = item
        tile_f = tile_set.astype(jnp.float32) * live_set[:, None, None].astype(jnp.float32)
        ahead = jnp.einsum('sij,sjd->sid', tile_f, fwd_blocks[col_ids])
        behind = jnp.einsum('sji,sjd->sid', tile_f, back_blocks[row_ids])
        return (acc_ahead.at[row_ids].add(ahead), acc_back.at[col_ids].add(behind)), None

    start = jnp.zeros((blocks, BS, D), jnp.float32)
    (ahead_sum, back_sum), _ = lax.scan(step, (start, start), (tiles, rows_glob, cols_glob, live))
    return ahead_sum.reshape(NODES, D), back_sum.reshape(NODES, D)


def reference(node_feats, grad_out, tile_weight, tile_row, src_block, tile_count, w_self, w_out, w_in):
    devices_all = N_WIDE * N_NARROW
    tiles = tile_weight.reshape(devices_all, TILES_DEV, BS, BS)
    slot = jnp.arange(TILES_DEV, dtype=jnp.int32)
    owner = slot // CAP
    narrow_ids = jnp.arange(N_NARROW, dtype=jnp.int32)[None, :, None]
    rows_glob = (narrow_ids * BPN + tile_row).astype(jnp.int32).reshape(devices_all, TILES_DEV)
    cols_glob = (owner[None, None, :] * BPN + src_block).astype(jnp.int32).reshape(devices_all, TILES_DEV)
    live = ((slot % CAP)[None, None, :] < jnp.repeat(tile_count, CAP, axis=2)).reshape(devices_all, TILES_DEV)
    agg_out, agg_in = spread(node_feats, node_feats, tiles, rows_glob, cols_glob, live)
    agg_out = agg_out.astype(jnp.bfloat16)
    agg_in = agg_in.astype(jnp.bfloat16)
    pre = (jnp.dot(node_feats, w_self, preferred_element_type=jnp.float32)
           + jnp.dot(agg_out, w_out, preferred_element_type=jnp.float32)
           + jnp.dot(agg_in, w_in, preferred_element_type=jnp.float32))
    sigma = jax.nn.sigmoid(pre)
    hidden = (pre * sigma).astype(jnp.bfloat16)
    grad_pre = (grad_out.astype(jnp.float32) * sigma * (1.0 + pre * (1.0 - sigma))).astype(jnp.bfloat16)
    grad_w_self = jnp.dot(node_feats.T, grad_pre, preferred_element_type=jnp.float32)
    grad_w_out = jnp.dot(agg_out.T, grad_pre, preferred_element_type=jnp.float32)
    grad_w_in = jnp.dot(agg_in.T, grad_pre, preferred_element_type=jnp.float32)
    grad_agg_out = jnp.dot(grad_pre, w_out.T, preferred_element_type=jnp.float32).astype(jnp.bfloat16)
    grad_agg_in = jnp.dot(grad_pre, w_in.T, preferred_element_type=jnp.float32).astype(jnp.bfloat16)
    grad_self = jnp.dot(grad_pre, w_self.T, preferred_element_type=jnp.float32)
    ahead_grad, back_grad = spread(grad_agg_in, grad_agg_out, tiles, rows_glob, cols_glob, live)
    grad_feats = (grad_self + back_grad + ahead_grad).astype(jnp.bfloat16)
    return hidden, grad_feats, grad_w_self, grad_w_out, grad_w_in
```

```python
import functools

import jax
import jax.numpy as jnp
from jax import lax
from jax.experimental import pallas as pl
from jax.experimental.pallas import tpu as pltpu
from jax.sharding import PartitionSpec as P

BF = jnp.bfloat16
F32 = jnp.float32
META = 16
CORES = 2


def dims(wide, narrow):
    z = 4 if narrow % 4 == 0 else 1
    return wide // CORES, z, narrow // z


def x_shift(a, k, wide):
    return lax.ppermute(a, "wide", [(i, (i + CORES * k) % wide) for i in range(wide)])


def core_swap(a, wide):
    return lax.ppermute(a, "wide", [(i, i ^ 1) for i in range(wide)])


def core_send(a, source, wide):
    return lax.ppermute(a, "wide", [(i, i ^ 1) for i in range(wide) if i % CORES == source])


def z_shift(a, zs, ys):
    return lax.ppermute(
        a, "narrow", [(z * ys + y, (z + 1) % zs * ys + y) for z in range(zs) for y in range(ys)]
    )


def y_shift(a, zs, ys):
    return lax.ppermute(
        a, "narrow", [(z * ys + y, z * ys + (y + 1) % ys) for z in range(zs) for y in range(ys)]
    )


def gather_narrow(piece, zs, ys):
    pieces = {}
    held = piece
    for k in range(zs):
        pieces[k, 0] = held
        if k < zs - 1:
            held = z_shift(held, zs, ys)
    for k in range(zs):
        for j in range(1, ys):
            pieces[k, j] = y_shift(pieces[k, j - 1], zs, ys)
    return [pieces[k, j] for k in range(zs) for j in range(ys)]


def aggregate_kernel(
    wide, narrow, cap, blocks, side, rr, xx, order, core, *refs
):
    half = blocks // CORES
    rows = refs[:wide]
    cols = refs[wide : 2 * wide]
    mine = refs[2 * wide : 2 * wide + narrow]
    other = refs[2 * wide + narrow : 2 * wide + 2 * narrow]
    out_ref, tiles, feats, acc, tile_sem, feat_sem = refs[2 * wide + 2 * narrow :]

    def tile_copy(source, w):
        return pltpu.make_async_copy(source[w], tiles.at[w], tile_sem.at[w])

    @pl.when(core[0] == 0)
    def _():
        for w in range(wide):
            tile_copy(rows, w).start()

    @pl.when(core[0] == 1)
    def _():
        for w in range(wide):
            tile_copy(cols, w).start()

    copies = []
    for q in range(narrow):
        for h, source in enumerate((mine, other)):
            copy = pltpu.make_async_copy(
                source[q],
                feats.at[pl.ds(q * blocks + h * half, half)],
                feat_sem.at[q * CORES + h],
            )
            copy.start()
            copies.append(copy)
    acc[...] = jnp.zeros_like(acc)
    for w in range(wide):
        tile_copy(rows, w).wait()
    for q in range(narrow):
        copies[CORES * q].wait()
        copies[CORES * q + 1].wait()
        owner = order[q]

        def step(w, carry):
            base = (w * narrow + owner) * cap
            terms = []
            for i in range(cap):
                terms.append(
                    jnp.dot(
                        tiles[w, owner, i * side : (i + 1) * side, :],
                        feats[q * blocks + xx[base + i]],
                        preferred_element_type=F32,
                    )
                )
            for i in range(cap):
                row = rr[base + i]
                acc[row] = acc[row] + terms[i]
            return carry

        lax.fori_loop(0, wide, step, 0)
    for b in range(blocks):
        out_ref[b * side : (b + 1) * side, :] = acc[b].astype(BF)


def aggregate(rr, xx, order, core, rows, cols, mine, other, blocks, side, cap):
    wide, narrow = len(rows), len(mine)
    width = mine[0].shape[-1]
    any_spec = pl.BlockSpec(memory_space=pl.ANY)
    smem = pl.BlockSpec(memory_space=pltpu.SMEM)
    return pl.pallas_call(
        functools.partial(aggregate_kernel, wide, narrow, cap, blocks, side),
        out_shape=jax.ShapeDtypeStruct((blocks * side, width), BF),
        in_specs=[smem] * 4 + [any_spec] * (2 * wide + 2 * narrow),
        out_specs=pl.BlockSpec(memory_space=pltpu.VMEM),
        scratch_shapes=[
            pltpu.VMEM((wide,) + rows[0].shape, BF),
            pltpu.VMEM((narrow * blocks, side, width), BF),
            pltpu.VMEM((blocks + 1, side, width), F32),
            pltpu.SemaphoreType.DMA((wide,)),
            pltpu.SemaphoreType.DMA((CORES * narrow,)),
        ],
        compiler_params=pltpu.CompilerParams(vmem_limit_bytes=56 << 20),
    )(rr, xx, order, core, *rows, *cols, *mine, *other)


def linear_sum(parts, weights, dims_):
    total = None
    for part, weight in zip(parts, weights):
        term = lax.dot_general(part, weight, dims_, preferred_element_type=F32)
        total = term if total is None else total + term
    return total


PLAIN = (((1,), (0,)), ((), ()))


def layer_kernel(parts, *refs):
    ins = refs[:parts]
    cotangent = refs[parts]
    weights = refs[parts + 1 : 2 * parts + 1]
    hidden_ref, grad_ref = refs[2 * parts + 1 :]
    pre = linear_sum([r[...] for r in ins], [r[...] for r in weights], PLAIN)
    sigma = 1.0 / (1.0 + jnp.exp(-pre))
    hidden_ref[...] = (pre * sigma).astype(BF)
    grad_ref[...] = (cotangent[...].astype(F32) * sigma * (1.0 + pre * (1.0 - sigma))).astype(BF)


def final_kernel(parts, *refs):
    ins = refs[:parts]
    weights = refs[parts : 2 * parts]
    out_ref = refs[2 * parts]
    out_ref[...] = linear_sum([r[...] for r in ins], [r[...] for r in weights], PLAIN).astype(BF)


def row_specs(arrays, step):
    return [pl.BlockSpec((step, a.shape[1]), lambda i: (i, 0)) for a in arrays]


def whole_specs(arrays):
    return [pl.BlockSpec(a.shape, lambda i: (0, 0)) for a in arrays]


def layer(ins, cotangent, weights, step):
    rows, width = cotangent.shape
    shape = jax.ShapeDtypeStruct((rows, width), BF)
    return pl.pallas_call(
        functools.partial(layer_kernel, len(ins)),
        grid=(rows // step,),
        out_shape=(shape, shape),
        in_specs=row_specs(list(ins) + [cotangent], step) + whole_specs(weights),
        out_specs=tuple(row_specs([cotangent, cotangent], step)),
        compiler_params=pltpu.CompilerParams(vmem_limit_bytes=40 << 20),
    )(*ins, cotangent, *weights)


def final(ins, weights, step):
    rows, width = ins[0].shape[0], weights[0].shape[1]
    return pl.pallas_call(
        functools.partial(final_kernel, len(ins)),
        grid=(rows // step,),
        out_shape=jax.ShapeDtypeStruct((rows, width), BF),
        in_specs=row_specs(ins, step) + whole_specs(weights),
        out_specs=pl.BlockSpec((step, width), lambda i: (i, 0)),
        compiler_params=pltpu.CompilerParams(vmem_limit_bytes=40 << 20),
    )(*ins, *weights)


def body(node_feats, grad_out, tile_weight, tile_row, src_block, tile_count, w_self, w_out, w_in):
    wide, narrow = lax.axis_size("wide"), lax.axis_size("narrow")
    xs, zs, ys = dims(wide, narrow)
    slots = tile_row.shape[-1]
    cap = slots // narrow
    nodes, width = node_feats.shape
    side = tile_weight.shape[-1]
    blocks = nodes // side
    half = blocks // CORES
    cols = width // xs
    step = nodes // 7
    w_id, n_id = lax.axis_index("wide"), lax.axis_index("narrow")
    core, x_id = w_id % CORES, w_id // CORES
    z_id, y_id = n_id // ys, n_id % ys

    tiles = tile_weight.reshape(narrow, cap, side, side)
    live = jnp.arange(cap, dtype=jnp.int32)[None, :] < tile_count.reshape(narrow, 1)
    facts = jnp.stack(
        [
            tile_row.reshape(narrow, cap).astype(BF),
            src_block.reshape(narrow, cap).astype(BF),
            live.astype(BF),
        ],
        axis=1,
    )
    facts = jnp.pad(facts, ((0, 0), (0, META - 3), (0, side - cap)))

    def packed(t):
        return jnp.concatenate([t.reshape(narrow, cap * side, side), facts], axis=1)

    row_own = packed(tiles)
    col_own = lax.all_to_all(
        packed(tiles.swapaxes(2, 3)), "narrow", split_axis=0, concat_axis=0, tiled=True
    )
    row_sets = [row_own] + [x_shift(row_own, k, wide) for k in range(1, xs)]
    col_sets = [col_own] + [x_shift(col_own, k, wide) for k in range(1, xs)]
    row_sets += [core_send(a, 1, wide) for a in row_sets]
    col_sets += [core_send(a, 0, wide) for a in col_sets]

    def fact(sets, i):
        return jnp.stack([a[:, cap * side + i, :cap] for a in sets]).astype(jnp.int32)

    row_f = [fact(row_sets, i) for i in range(3)]
    col_f = [fact(col_sets, i) for i in range(3)]
    first = core == 0
    to_block = jnp.where(first, row_f[0], col_f[1])
    from_block = jnp.where(first, row_f[1], col_f[0])
    alive = jnp.where(first, row_f[2], col_f[2])
    rr = jnp.where(alive > 0, to_block, blocks).reshape(-1)
    xx = (jnp.where(from_block // half == core, 0, half) + from_block % half).reshape(-1)
    q = jnp.arange(narrow, dtype=jnp.int32)
    order = ((z_id - q // ys) % zs * ys + (y_id - q % ys) % ys).astype(jnp.int32)
    core_arr = core.reshape(1).astype(jnp.int32)

    def spread(a):
        piece = lax.dynamic_slice(a, (core * half * side, x_id * cols), (half * side, cols))
        mine = gather_narrow(piece.reshape(half, side, cols), zs, ys)
        other = [core_swap(p, wide) for p in mine]
        own = aggregate(
            rr, xx, order, core_arr, row_sets, col_sets, mine, other, blocks, side, cap
        )
        here = [own] + [x_shift(own, k, wide) for k in range(1, xs)]
        return own, here + [core_swap(p, wide) for p in here]

    def weight_parts(first_w, second_w):
        own_w = jnp.where(first, first_w, second_w)
        oth_w = jnp.where(first, second_w, first_w)
        at = [(x_id - k) % xs * cols for k in range(xs)]
        return [
            lax.dynamic_slice(w, (a, 0), (cols, width)) for w in (own_w, oth_w) for a in at
        ]

    own, aggs = spread(node_feats)
    hidden, grad_pre = layer(
        [node_feats] + aggs, grad_out, [w_self] + weight_parts(w_out, w_in), step
    )
    over_rows = (((0,), (0,)), ((), ()))
    share = width // wide
    feat_part = lax.dynamic_slice(node_feats, (0, w_id * share), (nodes, share))
    grad_part = jnp.concatenate(
        [
            lax.dot_general(own, grad_pre, over_rows, preferred_element_type=F32),
            lax.dot_general(feat_part, grad_pre, over_rows, preferred_element_type=F32),
        ],
        axis=0,
    )
    for pairs in narrow_swaps(narrow):
        grad_part = grad_part + lax.ppermute(grad_part, "narrow", pairs)
    x_parts = [grad_part] + [x_shift(grad_part, k, wide) for k in range(1, xs)]
    stack = jnp.stack(x_parts)
    stack = jnp.stack([stack, core_swap(stack, wide)])
    stack = jnp.where(first, stack, stack[::-1])
    chip = (x_id - jnp.arange(xs)) % xs
    stack = stack[:, chip] if xs > 1 else stack
    agg_grads = stack[:, :, :cols].reshape(CORES, width, width)
    grad_ws = stack[:, :, cols:].swapaxes(0, 1).reshape(width, width)

    _, backs = spread(grad_pre)
    grad_feats = final(
        [grad_pre] + backs, [w_self.T] + weight_parts(w_in.T, w_out.T), step
    )
    return (hidden, grad_feats, grad_ws, agg_grads[0], agg_grads[1])


def narrow_swaps(narrow):
    bit = 1
    while bit < narrow:
        yield [(i, i ^ bit) for i in range(narrow)]
        bit *= 2


def solution(mesh):
    return jax.shard_map(
        body,
        mesh=mesh,
        in_specs=(
            P("narrow", None),
            P("narrow", None),
            P("wide", "narrow", None, None, None),
            P("wide", "narrow", None),
            P("wide", "narrow", None),
            P("wide", "narrow", None),
            P(),
            P(),
            P(),
        ),
        out_specs=(P("narrow", None), P("narrow", None), P(), P(), P()),
        check_vma=False,
    )
```

```python
import functools

import jax
import jax.numpy as jnp
from jax import lax
from jax.experimental import pallas as pl
from jax.experimental.pallas import tpu as pltpu
from jax.sharding import PartitionSpec as P

BF = jnp.bfloat16
F32 = jnp.float32
META = 16
CORES = 2


def dims(wide, narrow):
    z = 4 if narrow % 4 == 0 else 1
    return wide // CORES, z, narrow // z


def x_shift(a, k, wide):
    return lax.ppermute(a, "wide", [(i, (i + CORES * k) % wide) for i in range(wide)])


def core_swap(a, wide):
    return lax.ppermute(a, "wide", [(i, i ^ 1) for i in range(wide)])


def to_core(a, source, target, k, wide):
    return lax.ppermute(
        a,
        "wide",
        [(i, ((i // CORES + k) * CORES + target) % wide) for i in range(source, wide, CORES)],
    )


def z_shift(a, k, zs, ys):
    return lax.ppermute(
        a, "narrow", [(z * ys + y, (z + k) % zs * ys + y) for z in range(zs) for y in range(ys)]
    )


def y_shift(a, k, zs, ys):
    return lax.ppermute(
        a, "narrow", [(z * ys + y, z * ys + (y + k) % ys) for z in range(zs) for y in range(ys)]
    )


def after(a, *others):
    return lax.optimization_barrier((a,) + others)[0]


def aggregate_kernel(wide, cap, side, blocks, qs, layout, last, scal, *refs):
    half = blocks // CORES
    refs = list(refs)
    row_sets = [refs.pop(0) for _ in range(wide)]
    col_sets = [[refs.pop(0) for _ in part] for part in layout["cols"]]
    mine = [[refs.pop(0) for _ in range(layout["split"][q])] for q in qs]
    other = [[refs.pop(0) for _ in range(layout["split"][q])] for q in qs]
    acc_in = refs.pop(0) if layout["carry"] else None
    out_ref, tiles, feats, acc, facts_v, facts_s, tile_sem, feat_sem, sem = refs
    narrow = layout["narrow"]

    if acc_in is not None:
        carried = pltpu.make_async_copy(acc_in, acc, sem.at[0])
        carried.start()

    def row_copy(n, w):
        return pltpu.make_async_copy(
            row_sets[w].at[scal[1 + qs[n]]], tiles.at[n * wide + w], tile_sem.at[n * wide + w]
        )

    def col_copy(n, w):
        part, start = layout["where"][qs[n]]
        return pltpu.make_async_copy(
            col_sets[w][part].at[qs[n] - start],
            tiles.at[n * wide + w],
            tile_sem.at[n * wide + w],
        )

    @pl.when(scal[0] == 0)
    def _():
        for n in range(len(qs)):
            for w in range(wide):
                row_copy(n, w).start()

    @pl.when(scal[0] != 0)
    def _():
        for n in range(len(qs)):
            for w in range(wide):
                col_copy(n, w).start()

    copies = []
    for n in range(len(qs)):
        here = []
        for h, group in enumerate((mine[n], other[n])):
            size = half // len(group)
            for e, source in enumerate(group):
                copy = pltpu.make_async_copy(
                    source,
                    feats.at[pl.ds(n * blocks + h * half + e * size, size)],
                    feat_sem.at[(n * CORES + h) * 2 + e],
                )
                copy.start()
                here.append(copy)
        copies.append(here)
    if acc_in is None:
        acc[...] = jnp.zeros_like(acc)
    for n in range(len(qs)):
        for w in range(wide):
            row_copy(n, w).wait()
    core = scal[0]
    facts = tiles[:, cap * side : cap * side + META, :].astype(F32)
    row = facts[:, 0, :].astype(jnp.int32)
    source = facts[:, 1, :].astype(jnp.int32)
    alive = facts[:, 2, :] > 0.5
    to_block = jnp.where(core == 0, row, source)
    from_block = jnp.where(core == 0, source, row)
    upper = (from_block >= half).astype(jnp.int32)
    facts_v[0] = jnp.where(alive, to_block, blocks)
    facts_v[1] = from_block - upper * half + jnp.where(upper == core, 0, half)
    scalars = pltpu.make_async_copy(facts_v, facts_s, sem.at[1])
    scalars.start()
    scalars.wait()
    if acc_in is not None:
        carried.wait()
    for n in range(len(qs)):
        for copy in copies[n]:
            copy.wait()
        for w in range(wide):
            t = n * wide + w
            terms = []
            for i in range(cap):
                terms.append(
                    jnp.dot(
                        tiles[t, i * side : (i + 1) * side, :],
                        feats[n * blocks + facts_s[1, t, i]],
                        preferred_element_type=F32,
                    )
                )
            for i in range(cap):
                to = facts_s[0, t, i]
                acc[to] = acc[to] + terms[i]
    if last:
        for b in range(blocks):
            out_ref[b * side : (b + 1) * side, :] = acc[b].astype(BF)
    else:
        out_ref[...] = acc[...]


def aggregate(scal, row_sets, col_sets, where, mine, other, qs, carry, last, blocks, side, cap):
    wide = len(row_sets)
    width = mine[qs[0]][0].shape[-1]
    narrow = row_sets[0].shape[0]
    layout = dict(
        cols=[[0] * len(c) for c in col_sets],
        where=where,
        split={q: len(mine[q]) for q in qs},
        carry=carry is not None,
        narrow=narrow,
    )
    operands = list(row_sets) + [a for c in col_sets for a in c]
    operands += [a for q in qs for a in mine[q]] + [a for q in qs for a in other[q]]
    if carry is not None:
        operands.append(carry)
    count = len(qs) * wide
    if last:
        shape = jax.ShapeDtypeStruct((blocks * side, width), BF)
    else:
        shape = jax.ShapeDtypeStruct((blocks + 1, side, width), F32)
    flops = 2 * count * cap * side * side * width
    return pl.pallas_call(
        functools.partial(aggregate_kernel, wide, cap, side, blocks, qs, layout, last),
        out_shape=shape,
        in_specs=[pl.BlockSpec(memory_space=pltpu.SMEM)]
        + [pl.BlockSpec(memory_space=pl.ANY)] * len(operands),
        out_specs=pl.BlockSpec(memory_space=pltpu.VMEM),
        scratch_shapes=[
            pltpu.VMEM((count,) + row_sets[0].shape[1:], BF),
            pltpu.VMEM((len(qs) * blocks, side, width), BF),
            pltpu.VMEM((blocks + 1, side, width), F32),
            pltpu.VMEM((2, count, side), jnp.int32),
            pltpu.SMEM((2, count, side), jnp.int32),
            pltpu.SemaphoreType.DMA((count,)),
            pltpu.SemaphoreType.DMA((len(qs) * CORES * 2,)),
            pltpu.SemaphoreType.DMA((2,)),
        ],
        compiler_params=pltpu.CompilerParams(vmem_limit_bytes=58 << 20),
        cost_estimate=pl.CostEstimate(
            flops=flops, bytes_accessed=count * cap * side * side * 6, transcendentals=0
        ),
    )(scal, *operands)


def joined_dot(parts, weight):
    return jnp.dot(
        jnp.concatenate([r[...] for r in parts], axis=1), weight[...], preferred_element_type=F32
    )


def layer_kernel(parts, *refs):
    ins = refs[:parts]
    cotangent, weight, hidden_ref, grad_ref = refs[parts:]
    pre = joined_dot(ins, weight)
    sigma = 1.0 / (1.0 + jnp.exp(-pre))
    hidden_ref[...] = (pre * sigma).astype(BF)
    grad_ref[...] = (cotangent[...].astype(F32) * sigma * (1.0 + pre * (1.0 - sigma))).astype(BF)


def final_kernel(parts, *refs):
    ins = refs[:parts]
    weight, out_ref = refs[parts:]
    out_ref[...] = joined_dot(ins, weight).astype(BF)


def row_specs(arrays, step):
    return [pl.BlockSpec((step, a.shape[1]), lambda i: (i, 0)) for a in arrays]


def layer(ins, cotangent, weight, step):
    rows, width = cotangent.shape
    shape = jax.ShapeDtypeStruct((rows, width), BF)
    return pl.pallas_call(
        functools.partial(layer_kernel, len(ins)),
        grid=(rows // step,),
        out_shape=(shape, shape),
        in_specs=row_specs(list(ins) + [cotangent], step)
        + [pl.BlockSpec(weight.shape, lambda i: (0, 0))],
        out_specs=tuple(row_specs([cotangent, cotangent], step)),
        compiler_params=pltpu.CompilerParams(vmem_limit_bytes=58 << 20),
    )(*ins, cotangent, weight)


def final(ins, weight, step):
    rows, width = ins[0].shape[0], weight.shape[1]
    return pl.pallas_call(
        functools.partial(final_kernel, len(ins)),
        grid=(rows // step,),
        out_shape=jax.ShapeDtypeStruct((rows, width), BF),
        in_specs=row_specs(ins, step) + [pl.BlockSpec(weight.shape, lambda i: (0, 0))],
        out_specs=pl.BlockSpec((step, width), lambda i: (i, 0)),
        compiler_params=pltpu.CompilerParams(vmem_limit_bytes=58 << 20),
    )(*ins, weight)


def body(node_feats, grad_out, tile_weight, tile_row, src_block, tile_count, w_self, w_out, w_in):
    wide, narrow = lax.axis_size("wide"), lax.axis_size("narrow")
    xs, zs, ys = dims(wide, narrow)
    slots = tile_row.shape[-1]
    cap = slots // narrow
    nodes, width = node_feats.shape
    side = tile_weight.shape[-1]
    blocks = nodes // side
    half = blocks // CORES
    cols = width // xs
    step = nodes // 7
    w_id, n_id = lax.axis_index("wide"), lax.axis_index("narrow")
    core, x_id = w_id % CORES, w_id // CORES
    z_id, y_id = n_id // ys, n_id % ys
    first = core == 0
    every = [(k, j) for k in range(zs) for j in range(ys)]

    def own_piece(a):
        piece = lax.dynamic_slice(a, (core * half * side, x_id * cols), (half * side, cols))
        return piece.reshape(half, side, cols)

    tiles = tile_weight.reshape(narrow, cap, side, side)
    live = jnp.arange(cap, dtype=jnp.int32)[None, :] < tile_count.reshape(narrow, 1)
    facts = jnp.stack(
        [
            tile_row.reshape(narrow, cap).astype(BF),
            src_block.reshape(narrow, cap).astype(BF),
            live.astype(BF),
        ],
        axis=1,
    )
    facts = jnp.pad(facts, ((0, 0), (0, META - 3), (0, side - cap)))

    def packed(t):
        return jnp.concatenate([t.reshape(narrow, cap * side, side), facts], axis=1)

    row_own = packed(tiles)
    col_by_owner = packed(tiles.swapaxes(2, 3)).reshape(zs, ys, cap * side + META, side)
    q = jnp.arange(narrow, dtype=jnp.int32)
    order = (z_id - q // ys) % zs * ys + (y_id - q % ys) % ys
    scal = jnp.concatenate([core.reshape(1), order]).astype(jnp.int32)

    feats = {(0, 0): own_piece(node_feats)}
    toward = [
        lax.dynamic_index_in_dim(col_by_owner, (y_id + j) % ys, 1, keepdims=False)
        for j in range(ys)
    ]
    moved = [toward[0]] + [y_shift(toward[j], j, zs, ys) for j in range(1, ys)]
    row_sets = [row_own, to_core(row_own, 1, 0, 0, wide)]
    for k in range(1, xs):
        row_sets += [to_core(row_own, c, 0, k, wide) for c in range(CORES)]
    feats[1, 0] = z_shift(feats[0, 0], 1, zs, ys)
    feats[0, 1] = y_shift(after(feats[0, 0], *moved[1:]), 1, zs, ys)
    col_by_z = jnp.stack(moved, axis=1)

    def col_shift(k, *ahead):
        part = lax.dynamic_index_in_dim(col_by_z, (z_id + k) % zs, 0, keepdims=False)
        return z_shift(after(part, *ahead), k, zs, ys) if k else part

    col_parts = [col_shift(0), col_shift(1)]
    feats[2, 0] = z_shift(after(feats[1, 0]), 1, zs, ys)
    feats[1, 1] = y_shift(after(feats[1, 0], feats[0, 1]), 1, zs, ys)
    col_parts.append(col_shift(2, feats[2, 0]))
    feats[3, 0] = z_shift(after(feats[2, 0], col_parts[1]), 1, zs, ys)
    feats[2, 1] = y_shift(after(feats[2, 0], feats[1, 1]), 1, zs, ys)
    col_parts.append(col_shift(3, col_parts[2]))
    feats[3, 1] = y_shift(after(feats[3, 0], feats[2, 1]), 1, zs, ys)
    for k in range(zs):
        for j in range(2, ys):
            feats[k, j] = y_shift(feats[k, j - 1], 1, zs, ys)
    early_cols = jnp.concatenate(col_parts[:3], axis=0)
    late_cols = col_parts[3]

    def col_sources(a):
        sets = [a, to_core(a, 0, 1, 0, wide)]
        for k in range(1, xs):
            sets += [to_core(a, c, 1, k, wide) for c in range(CORES)]
        return sets

    col_sets = [list(pair) for pair in zip(col_sources(early_cols), col_sources(late_cols))]
    cut = 3 * ys
    where = {i: (0, 0) if i < cut else (1, cut) for i in range(narrow)}

    def spread(pieces):
        mine = [pieces[kj] if isinstance(pieces[kj], list) else [pieces[kj]] for kj in every]
        other = [[core_swap(p, wide) for p in group] for group in mine]
        late = [i for i, kj in enumerate(every) if kj[0] == 3 or kj[0] == 2 and kj[1] > 0]
        soon = [i for i in range(narrow) if i not in late]
        args = (mine, other)
        carry = aggregate(
            scal, row_sets, [c[:1] for c in col_sets], where, *args, soon, None, False,
            blocks, side, cap,
        )
        own = aggregate(
            scal, row_sets, col_sets, where, *args, late, carry, True, blocks, side, cap
        )
        here = [own] + [x_shift(own, k, wide) for k in range(1, xs)]
        return own, here + [core_swap(p, wide) for p in here]

    def stacked(self_w, first_w, second_w):
        own_w = jnp.where(first, first_w, second_w)
        oth_w = jnp.where(first, second_w, first_w)
        at = [(x_id - k) % xs * cols for k in range(xs)]
        return jnp.concatenate(
            [self_w]
            + [lax.dynamic_slice(w, (a, 0), (cols, width)) for w in (own_w, oth_w) for a in at],
            axis=0,
        )

    own, aggs = spread(feats)
    hidden, grad_pre = layer(
        [node_feats] + aggs, grad_out, stacked(w_self, w_out, w_in), step
    )

    grads = {(0, 0): own_piece(grad_pre)}
    grads[1, 0] = z_shift(grads[0, 0], 1, zs, ys)
    grads[0, 1] = y_shift(grads[0, 0], 1, zs, ys)
    over_rows = (((0,), (0,)), ((), ()))
    share = width // wide
    feat_part = lax.dynamic_slice(node_feats, (0, w_id * share), (nodes, share))
    grad_part = lax.dot_general(
        jnp.concatenate([own, feat_part], axis=1), grad_pre, over_rows, preferred_element_type=F32
    )
    grads[2, 0] = z_shift(after(grads[1, 0], grads[0, 1]), 1, zs, ys)
    grads[1, 1] = y_shift(after(grads[1, 0], grads[0, 1]), 1, zs, ys)
    grads[3, 0] = z_shift(after(grads[2, 0], grads[1, 1]), 1, zs, ys)
    grads[2, 1] = y_shift(after(grads[2, 0], grads[1, 1]), 1, zs, ys)
    for k in range(zs):
        for j in range(1, ys):
            if (k, j) not in grads and (k < 3 or j > 1):
                if k == 3 and ys > 2:
                    continue
                grads[k, j] = y_shift(grads[k, j - 1], 1, zs, ys)
    quarter = half // 2
    for j in range(1, ys):
        before = grads[3, j - 1]
        before = jnp.concatenate(before, axis=0) if isinstance(before, list) else before
        ready = grads[2, 1]
        grads[3, j] = [
            y_shift(after(before[:quarter], ready), 1, zs, ys),
            z_shift(grads[2, j][quarter:], 1, zs, ys),
        ]
    _, backs = spread(grads)

    for pairs in narrow_swaps(narrow):
        grad_part = grad_part + lax.ppermute(grad_part, "narrow", pairs)
    x_parts = [grad_part] + [x_shift(grad_part, k, wide) for k in range(1, xs)]
    stack = jnp.stack(x_parts)
    stack = jnp.stack([stack, core_swap(stack, wide)])
    stack = jnp.where(first, stack, stack[::-1])
    if xs == 2:
        stack = jnp.where(x_id == 0, stack, stack[:, ::-1])
    else:
        stack = stack[:, (x_id - jnp.arange(xs)) % xs]
    agg_grads = stack[:, :, :cols].reshape(CORES, width, width)
    grad_ws = stack[:, :, cols:].swapaxes(0, 1).reshape(width, width)

    grad_feats = final([grad_pre] + backs, stacked(w_self.T, w_in.T, w_out.T), step)
    return (hidden, grad_feats, grad_ws, agg_grads[0], agg_grads[1])


def narrow_swaps(narrow):
    bit = 1
    while bit < narrow:
        yield [(i, i ^ bit) for i in range(narrow)]
        bit *= 2


def solution(mesh):
    return jax.shard_map(
        body,
        mesh=mesh,
        in_specs=(
            P("narrow", None),
            P("narrow", None),
            P("wide", "narrow", None, None, None),
            P("wide", "narrow", None),
            P("wide", "narrow", None),
            P("wide", "narrow", None),
            P(),
            P(),
            P(),
        ),
        out_specs=(P("narrow", None), P("narrow", None), P(), P(), P()),
        check_vma=False,
    )
```

```python
import functools

import jax
import jax.numpy as jnp
from jax import lax
from jax.experimental import pallas as pl
from jax.experimental.pallas import tpu as pltpu
from jax.sharding import PartitionSpec as P

BF = jnp.bfloat16
F32 = jnp.float32
META = 16
CORES = 2


def dims(wide, narrow):
    z = 4 if narrow % 4 == 0 else 1
    return wide // CORES, z, narrow // z


def x_shift(a, k, wide):
    return lax.ppermute(a, "wide", [(i, (i + CORES * k) % wide) for i in range(wide)])


def core_swap(a, wide):
    return lax.ppermute(a, "wide", [(i, i ^ 1) for i in range(wide)])


def z_shift(a, k, zs, ys):
    return lax.ppermute(
        a, "narrow", [(z * ys + y, (z + k) % zs * ys + y) for z in range(zs) for y in range(ys)]
    )


def y_shift(a, k, zs, ys):
    return lax.ppermute(
        a, "narrow", [(z * ys + y, z * ys + (y + k) % ys) for z in range(zs) for y in range(ys)]
    )


def after(a, *others):
    return lax.optimization_barrier((a,) + others)[0]


def aggregate_kernel(wide, cap, side, blocks, layout, scal, *refs):
    qs = range(layout["narrow"])
    half = blocks // CORES
    refs = list(refs)
    arrays = [refs.pop(0) for _ in range(layout["arrays"])]
    row_sets, col_sets = layout["rows"], layout["cols"]
    out_ref, tiles, feats, acc, facts_v, facts_s, tile_sem, feat_sem, sem = refs

    def take(place):
        at, index = place
        return arrays[at] if index is None else arrays[at].at[index]

    def col_copy(n, w):
        part, start = layout["where"][n]
        return pltpu.make_async_copy(
            take(col_sets[w][part]).at[start],
            tiles.at[n * wide + w],
            tile_sem.at[n * wide + w],
        )

    @pl.when(scal[0] == 0)
    def _():
        for n in range(len(qs)):
            owner = scal[2 + n]
            for w in range(wide):
                low, high = (take(r) for r in row_sets[w])
                into, done = tiles.at[n * wide + w], tile_sem.at[n * wide + w]
                if row_sets[w][0] == row_sets[w][1]:
                    pltpu.make_async_copy(low.at[owner], into, done).start()
                else:
                    split = len(qs) // 2

                    @pl.when(owner < split)
                    def _():
                        pltpu.make_async_copy(low.at[owner], into, done).start()

                    @pl.when(owner >= split)
                    def _():
                        pltpu.make_async_copy(high.at[owner - split], into, done).start()

    @pl.when(scal[0] != 0)
    def _():
        for n in range(len(qs)):
            for w in range(wide):
                col_copy(n, w).start()

    copies = []
    for n in range(len(qs)):
        here = []
        for h, group in enumerate(layout["feats"][n]):
            size = half // len(group)
            for e, place in enumerate(group):
                source = take(place)
                copy = pltpu.make_async_copy(
                    source,
                    feats.at[pl.ds(n * blocks + h * half + e * size, size)],
                    feat_sem.at[(n * CORES + h) * 2 + e],
                )
                copy.start()
                here.append(copy)
        copies.append(here)
    acc[...] = jnp.zeros_like(acc)
    for n in range(len(qs)):
        for w in range(wide):
            col_copy(n, w).wait()
    core = scal[0]
    facts = tiles[:, cap * side : cap * side + META, :].astype(F32)
    row = facts[:, 0, :].astype(jnp.int32)
    source = facts[:, 1, :].astype(jnp.int32)
    alive = facts[:, 2, :] > 0.5
    to_block = jnp.where(core == 0, row, source)
    from_block = jnp.where(core == 0, source, row)
    upper = (from_block >= half).astype(jnp.int32)
    facts_v[0] = jnp.where(alive, to_block, blocks)
    facts_v[1] = from_block - upper * half + jnp.where(upper == core, 0, half)
    scalars = pltpu.make_async_copy(facts_v, facts_s, sem.at[0])
    scalars.start()
    scalars.wait()
    for n in range(len(qs)):
        for copy in copies[n]:
            copy.wait()
        for w in range(wide):
            t = n * wide + w
            terms = []
            for i in range(cap):
                terms.append(
                    jnp.dot(
                        tiles[t, i * side : (i + 1) * side, :],
                        feats[n * blocks + facts_s[1, t, i]],
                        preferred_element_type=F32,
                    )
                )
            for i in range(cap):
                to = facts_s[0, t, i]
                acc[to] = acc[to] + terms[i]
    for b in range(blocks):
        out_ref[b * side : (b + 1) * side, :] = acc[b].astype(BF)


def aggregate(scal, row_sets, col_sets, where, mine, other, blocks, side, cap):
    wide, narrow = len(row_sets), len(mine)
    qs = range(narrow)
    width = mine[0][0][0].shape[-1]
    arrays = []

    def place(array, index):
        for at, known in enumerate(arrays):
            if known is array:
                return at, index
        arrays.append(array)
        return len(arrays) - 1, index

    layout = dict(
        rows=[[place(a, None) for a in r] for r in row_sets],
        cols=[[place(a, None) for a in c] for c in col_sets],
        where=where,
        feats=[[[place(*p) for p in group] for group in (mine[q], other[q])] for q in qs],
        narrow=narrow,
    )
    layout["arrays"] = len(arrays)
    operands = list(arrays)
    count = len(qs) * wide
    shape = jax.ShapeDtypeStruct((blocks * side, width), BF)
    flops = 2 * count * cap * side * side * width
    return pl.pallas_call(
        functools.partial(aggregate_kernel, wide, cap, side, blocks, layout),
        out_shape=shape,
        in_specs=[pl.BlockSpec(memory_space=pltpu.SMEM)]
        + [pl.BlockSpec(memory_space=pl.ANY)] * len(operands),
        out_specs=pl.BlockSpec(memory_space=pltpu.VMEM),
        scratch_shapes=[
            pltpu.VMEM((count,) + row_sets[0][0].shape[-2:], BF),
            pltpu.VMEM((len(qs) * blocks, side, width), BF),
            pltpu.VMEM((blocks + 1, side, width), F32),
            pltpu.VMEM((2, count, side), jnp.int32),
            pltpu.SMEM((2, count, side), jnp.int32),
            pltpu.SemaphoreType.DMA((count,)),
            pltpu.SemaphoreType.DMA((len(qs) * CORES * 2,)),
            pltpu.SemaphoreType.DMA((1,)),
        ],
        compiler_params=pltpu.CompilerParams(vmem_limit_bytes=58 << 20),
        cost_estimate=pl.CostEstimate(
            flops=flops, bytes_accessed=count * cap * side * side * 6, transcendentals=0
        ),
    )(scal, *operands)


def fill_weights(scal, refs, scratch, cols, across):
    self_ref, out_ref, in_ref = refs
    width = self_ref.shape[0]
    xs = width // cols
    core, chip = scal[0], scal[1]

    def put(at, value):
        if across:
            scratch[:, at : at + value.shape[1]] = value
        else:
            scratch[at : at + value.shape[0], :] = value

    put(0, self_ref[...])
    for d in range(CORES):
        for k in range(xs):
            rank = lax.rem(chip - k + xs, xs)
            out_w, in_w = out_ref[0], in_ref[0]
            for e in range(1, xs):
                out_w = jnp.where(rank == e, out_ref[e], out_w)
                in_w = jnp.where(rank == e, in_ref[e], in_w)
            use_out = (core == 0) == (d == 0)
            put(width + (d * xs + k) * cols, jnp.where(use_out, out_w, in_w))


def dense_kernel(parts, outs, cols, chunks, across, scal, *refs):
    refs = list(refs)
    count = parts + outs - 1
    ins = [refs.pop(0) for _ in range(count)]
    weights = [refs.pop(0) for _ in range(3)]
    results = [refs.pop(0) for _ in range(outs)]
    here = [refs.pop(0) for _ in range(count)]
    made = [refs.pop(0) for _ in range(outs)]
    scratch, in_sem, out_sem = refs
    step = here[0].shape[0] // chunks

    def rows(c):
        return pl.ds(c * step, step)

    def load(c, i):
        return pltpu.make_async_copy(
            ins[i].at[rows(c)], here[i].at[rows(c)], in_sem.at[c * count + i]
        )

    def save(c, i):
        return pltpu.make_async_copy(
            made[i].at[rows(c)], results[i].at[rows(c)], out_sem.at[c * outs + i]
        )

    for c in range(chunks):
        for i in range(count):
            load(c, i).start()
    fill_weights(scal, weights, scratch, cols, across)
    dims_ = (((1,), (1 if across else 0,)), ((), ()))
    for c in range(chunks):
        for i in range(count):
            load(c, i).wait()
        both = jnp.concatenate([h[rows(c), :] for h in here[:parts]], axis=1)
        pre = lax.dot_general(both, scratch[...], dims_, preferred_element_type=F32)
        if outs == 1:
            made[0][rows(c), :] = pre.astype(BF)
        else:
            sigma = 1.0 / (1.0 + jnp.exp(-pre))
            made[0][rows(c), :] = (pre * sigma).astype(BF)
            slope = here[parts][rows(c), :].astype(F32) * sigma * (1.0 + pre * (1.0 - sigma))
            made[1][rows(c), :] = slope.astype(BF)
        for i in range(outs):
            save(c, i).start()
    for c in range(chunks):
        for i in range(outs):
            save(c, i).wait()


def whole(a):
    return pl.BlockSpec(a.shape, lambda: (0,) * a.ndim)


def dense(scal, ins, weights, cols, chunks, outs, across):
    rows, width = ins[0].shape
    xs = width // cols
    if across:
        split = [w.reshape(width, xs, cols).swapaxes(0, 1) for w in weights[1:]]
        scratch = (width, width * (1 + CORES))
    else:
        split = [w.reshape(xs, cols, width) for w in weights[1:]]
        scratch = (width * (1 + CORES), width)
    weights = [weights[0]] + split
    shape = jax.ShapeDtypeStruct((rows, width), BF)
    any_spec = pl.BlockSpec(memory_space=pl.ANY)
    result = pl.pallas_call(
        functools.partial(dense_kernel, 1 + CORES * xs, outs, cols, chunks, across),
        out_shape=(shape,) * outs,
        in_specs=[pl.BlockSpec(memory_space=pltpu.SMEM)]
        + [any_spec] * len(ins)
        + [whole(w) for w in weights],
        out_specs=(any_spec,) * outs,
        scratch_shapes=[pltpu.VMEM(a.shape, BF) for a in ins]
        + [pltpu.VMEM((rows, width), BF)] * outs
        + [
            pltpu.VMEM(scratch, BF),
            pltpu.SemaphoreType.DMA((chunks * len(ins),)),
            pltpu.SemaphoreType.DMA((chunks * outs,)),
        ],
        compiler_params=pltpu.CompilerParams(vmem_limit_bytes=58 << 20),
    )(scal, *ins, *weights)
    return result if outs > 1 else result[0]


def body(node_feats, grad_out, tile_weight, tile_row, src_block, tile_count, w_self, w_out, w_in):
    wide, narrow = lax.axis_size("wide"), lax.axis_size("narrow")
    xs, zs, ys = dims(wide, narrow)
    slots = tile_row.shape[-1]
    cap = slots // narrow
    nodes, width = node_feats.shape
    side = tile_weight.shape[-1]
    blocks = nodes // side
    half = blocks // CORES
    cols = width // xs
    w_id, n_id = lax.axis_index("wide"), lax.axis_index("narrow")
    core, x_id = w_id % CORES, w_id // CORES
    z_id, y_id = n_id // ys, n_id % ys
    first = core == 0
    every = [(k, j) for k in range(zs) for j in range(ys)]

    def own_piece(a):
        piece = lax.dynamic_slice(a, (core * half * side, x_id * cols), (half * side, cols))
        return piece.reshape(half, side, cols)

    tiles = tile_weight.reshape(narrow, cap, side, side)
    live = jnp.arange(cap, dtype=jnp.int32)[None, :] < tile_count.reshape(narrow, 1)
    facts = jnp.stack(
        [
            tile_row.reshape(narrow, cap).astype(BF),
            src_block.reshape(narrow, cap).astype(BF),
            live.astype(BF),
        ],
        axis=1,
    )
    facts = jnp.pad(facts, ((0, 0), (0, META - 3), (0, side - cap)))

    def packed(t):
        return jnp.concatenate([t.reshape(narrow, cap * side, side), facts], axis=1)

    q = jnp.arange(narrow, dtype=jnp.int32)
    order = (z_id - q // ys) % zs * ys + (y_id - q % ys) % ys
    scal = jnp.concatenate([core.reshape(1), x_id.reshape(1), order]).astype(jnp.int32)

    def here(arrays):
        return [(a, None) for a in arrays]

    def swap(a, *ahead):
        return core_swap(after(a, *ahead), wide)

    def meet(a, bit):
        return lax.ppermute(a, "narrow", [(i, i ^ bit) for i in range(narrow)])

    def along_x(a, *ahead):
        return [x_shift(after(a, *ahead), k, wide) for k in range(1, xs)]

    own = own_piece(node_feats)
    z1 = z_shift(own, 1, zs, ys)
    row_own = packed(after(tiles, own))
    row_x0 = along_x(row_own[: narrow // 2], own)
    col_by_owner = packed(after(tiles, row_own).swapaxes(2, 3))
    col_by_owner = col_by_owner.reshape(zs, ys, cap * side + META, side)
    toward = [
        lax.dynamic_index_in_dim(col_by_owner, (y_id + j) % ys, 1, keepdims=False)
        for j in range(ys)
    ]
    moved = [y_shift(toward[j], j, zs, ys) for j in range(1, ys)]
    one = [z1] + moved + row_x0
    col_by_z = jnp.stack([toward[0]] + [after(m, *one) for m in moved], axis=1)

    def col_part(k, *ahead):
        part = lax.dynamic_index_in_dim(col_by_z, (z_id + k) % zs, 0, keepdims=False)
        return after(part, *ahead)

    s1 = z_shift(col_part(1, *one), 1, zs, ys)
    s3 = z_shift(col_part(3, *one), 3, zs, ys)
    y0 = y_shift(after(own, *one), 1, zs, ys)
    row_x1 = along_x(row_own[narrow // 2 :], *one)
    row_swap = swap(row_own, *one)
    two = [s1, s3, y0, row_swap] + row_x1
    z2 = z_shift(after(z1, *two), 1, zs, ys)
    y1 = y_shift(after(z1, *two), 1, zs, ys)
    near = jnp.concatenate([col_part(0, *one), s1], axis=0)
    near_x = along_x(near, *two)
    own_swap, z1_swap = swap(own, *two), swap(z1, *two)
    three = [z2, y1, own_swap, z1_swap] + near_x
    z3 = z_shift(after(z2, *three), 1, zs, ys)
    y2 = y_shift(after(z2, *three), 1, zs, ys)
    s3_x = along_x(s3, *three)
    y0_swap = swap(y0, *three)
    row_x0_swap = [swap(a, *three) for a in row_x0]
    four = [z3, y2, y0_swap] + s3_x + row_x0_swap
    y3 = y_shift(after(z3, *four), 1, zs, ys)
    s2 = z_shift(col_part(2, *four), 2, zs, ys)
    z2_swap, y1_swap = swap(z2, *four), swap(y1, *four)
    row_x1_swap = [swap(a, *four) for a in row_x1]
    five = [y3, s2, z2_swap, y1_swap] + row_x1_swap
    s2_x = along_x(s2, *five)
    z3_swap, y2_swap = swap(z3, *five), swap(y2, *five)
    near_swap = [swap(a, *five) for a in [near] + near_x]
    six = [z3_swap, y2_swap] + s2_x + near_swap
    y3_swap = swap(y3, *six)
    s3_swap = [swap(a, *six) for a in [s3] + s3_x]
    s2_swap = [swap(a, *six) for a in [s2] + s2_x]

    row_sets = [[row_own, row_own]] + [list(p) for p in zip(row_x0, row_x1)]
    row_sets += [[row_swap, row_swap]] + [list(p) for p in zip(row_x0_swap, row_x1_swap)]
    col_sets = [list(p) for p in zip([near] + near_x, [s3] + s3_x, [s2] + s2_x)]
    col_sets += [list(p) for p in zip(near_swap, s3_swap, s2_swap)]
    where = {}
    for i, (k, j) in enumerate(every):
        where[i] = {0: (0, i), 1: (0, i), 2: (2, j), 3: (1, j)}[k]

    def spread(pieces, swaps):
        for kj in every:
            if kj not in pieces:
                pieces[kj] = y_shift(pieces[kj[0], kj[1] - 1], 1, zs, ys)
            if kj not in swaps:
                swaps[kj] = core_swap(pieces[kj], wide)
        own = aggregate(
            scal, row_sets, col_sets, where, [here([pieces[kj]]) for kj in every],
            [here([swaps[kj]]) for kj in every], blocks, side, cap,
        )
        all_own = [own] + along_x(own)
        return own, all_own + [core_swap(p, wide) for p in all_own]

    names = [(0, 0), (1, 0), (2, 0), (3, 0), (0, 1), (1, 1), (2, 1), (3, 1)]
    agg, aggs = spread(
        dict(zip(names, [own, z1, z2, z3, y0, y1, y2, y3])),
        dict(zip(names, [own_swap, z1_swap, z2_swap, z3_swap, y0_swap, y1_swap, y2_swap, y3_swap])),
    )
    hidden, grad_pre = dense(
        scal, [node_feats] + aggs + [grad_out], [w_self, w_out, w_in], cols, 4, 2, False
    )

    own = own_piece(grad_pre)
    z1 = z_shift(own, 1, zs, ys)
    y0 = y_shift(own, 1, zs, ys)
    share = width // wide
    feat_part = lax.dynamic_slice(node_feats, (0, w_id * share), (nodes, share))
    grad_part = lax.dot_general(
        jnp.concatenate([agg, feat_part], axis=1),
        after(grad_pre, own),
        (((0,), (0,)), ((), ())),
        preferred_element_type=F32,
    )
    one = [z1, y0]
    z2 = z_shift(after(z1, *one), 1, zs, ys)
    y1 = y_shift(after(z1, *one), 1, zs, ys)
    upper = n_id % 2
    halves = after(grad_part, *one).reshape(2, -1, width)
    sent = lax.dynamic_index_in_dim(halves, 1 - upper, 0, keepdims=False)
    kept = lax.dynamic_index_in_dim(halves, upper, 0, keepdims=False)
    grad_half = kept + meet(sent, 1)
    own_swap, z1_swap = swap(own, *one), swap(z1, *one)
    two = [z2, y1, own_swap, z1_swap, grad_half]
    z3 = z_shift(after(z2, *two), 1, zs, ys)
    y2 = y_shift(after(z2, *two), 1, zs, ys)
    y0_swap, z2_swap = swap(y0, *two), swap(z2, *two)
    for bit in (2, 8):
        if bit < narrow:
            grad_half = grad_half + meet(after(grad_half, *two), bit)
    three = [z3, y2, y0_swap, z2_swap, grad_half]
    quarter = half // 2
    y3 = y_shift(after(z3, *three)[:quarter], 1, zs, ys)
    y3_rest = z_shift(after(y2, *three)[quarter:], 1, zs, ys)
    grad_half = grad_half + meet(after(grad_half, *three), 4)
    y1_swap, z3_swap = swap(y1, *three), swap(z3, *three)
    four = [y3, y3_rest, y1_swap, z3_swap, grad_half]
    y3 = jnp.concatenate([y3, y3_rest], axis=0)
    y2_swap, y3_swap = swap(y2, *four), swap(y3, *four)
    stack = jnp.stack([grad_half] + along_x(grad_half, *four))
    _, backs = spread(
        dict(zip(names, [own, z1, z2, z3, y0, y1, y2, y3])),
        dict(zip(names, [own_swap, z1_swap, z2_swap, z3_swap, y0_swap, y1_swap, y2_swap, y3_swap])),
    )
    there = meet(stack, 1)
    stack = jnp.concatenate(
        [jnp.where(upper == 1, there, stack), jnp.where(upper == 1, stack, there)], axis=1
    )
    stack = jnp.stack([stack, core_swap(stack, wide)])
    stack = jnp.where(first, stack, stack[::-1])
    if xs == 2:
        stack = jnp.where(x_id == 0, stack, stack[:, ::-1])
    else:
        stack = stack[:, (x_id - jnp.arange(xs)) % xs]
    agg_grads = stack[:, :, :cols].reshape(CORES, width, width)
    grad_ws = stack[:, :, cols:].swapaxes(0, 1).reshape(width, width)

    grad_feats = dense(scal, [grad_pre] + backs, [w_self, w_in, w_out], cols, 4, 1, True)
    return (hidden, grad_feats, grad_ws, agg_grads[0], agg_grads[1])


def solution(mesh):
    return jax.shard_map(
        body,
        mesh=mesh,
        in_specs=(
            P("narrow", None),
            P("narrow", None),
            P("wide", "narrow", None, None, None),
            P("wide", "narrow", None),
            P("wide", "narrow", None),
            P("wide", "narrow", None),
            P(),
            P(),
            P(),
        ),
        out_specs=(P("narrow", None), P("narrow", None), P(), P(), P()),
        check_vma=False,
    )
```

```python
import functools

import jax
import jax.numpy as jnp
from jax import lax
from jax.experimental import pallas as pl
from jax.experimental.pallas import tpu as pltpu
from jax.sharding import PartitionSpec as P

BF = jnp.bfloat16
F32 = jnp.float32
META = 16
CORES = 2


def dims(wide, narrow):
    z = 4 if narrow % 4 == 0 else 1
    return wide // CORES, z, narrow // z


def x_shift(a, k, wide):
    return lax.ppermute(a, "wide", [(i, (i + CORES * k) % wide) for i in range(wide)])


def core_swap(a, wide):
    return lax.ppermute(a, "wide", [(i, i ^ 1) for i in range(wide)])


def z_shift(a, k, zs, ys):
    return lax.ppermute(
        a, "narrow", [(z * ys + y, (z + k) % zs * ys + y) for z in range(zs) for y in range(ys)]
    )


def y_shift(a, k, zs, ys):
    return lax.ppermute(
        a, "narrow", [(z * ys + y, z * ys + (y + k) % ys) for z in range(zs) for y in range(ys)]
    )


def after(a, *others):
    return lax.optimization_barrier((a,) + others)[0]


def aggregate_kernel(wide, cap, side, blocks, layout, scal, *refs):
    qs = range(layout["narrow"])
    half = blocks // CORES
    refs = list(refs)
    arrays = [refs.pop(0) for _ in range(layout["arrays"])]
    row_sets, col_sets = layout["rows"], layout["cols"]
    out_ref, tiles, feats, acc, facts_v, facts_s, tile_sem, feat_sem, sem = refs

    def take(place):
        at, index = place
        return arrays[at] if index is None else arrays[at].at[index]

    def col_copy(n, w):
        part, start = layout["where"][n]
        return pltpu.make_async_copy(
            take(col_sets[w][part]).at[start],
            tiles.at[n * wide + w],
            tile_sem.at[n * wide + w],
        )

    @pl.when(scal[0] == 0)
    def _():
        for n in range(len(qs)):
            owner = scal[2 + n]
            for w in range(wide):
                low, high = (take(r) for r in row_sets[w])
                into, done = tiles.at[n * wide + w], tile_sem.at[n * wide + w]
                if row_sets[w][0] == row_sets[w][1]:
                    pltpu.make_async_copy(low.at[owner], into, done).start()
                else:
                    split = len(qs) // 2

                    @pl.when(owner < split)
                    def _():
                        pltpu.make_async_copy(low.at[owner], into, done).start()

                    @pl.when(owner >= split)
                    def _():
                        pltpu.make_async_copy(high.at[owner - split], into, done).start()

    @pl.when(scal[0] != 0)
    def _():
        for n in range(len(qs)):
            for w in range(wide):
                col_copy(n, w).start()

    copies = []
    for n in range(len(qs)):
        here = []
        for h, group in enumerate(layout["feats"][n]):
            size = half // len(group)
            for e, place in enumerate(group):
                source = take(place)
                copy = pltpu.make_async_copy(
                    source,
                    feats.at[pl.ds(n * blocks + h * half + e * size, size)],
                    feat_sem.at[(n * CORES + h) * 2 + e],
                )
                copy.start()
                here.append(copy)
        copies.append(here)
    acc[...] = jnp.zeros_like(acc)
    for n in range(len(qs)):
        for w in range(wide):
            col_copy(n, w).wait()
    core = scal[0]
    facts = tiles[:, cap * side : cap * side + META, :].astype(F32)
    row = facts[:, 0, :].astype(jnp.int32)
    source = facts[:, 1, :].astype(jnp.int32)
    alive = facts[:, 2, :] > 0.5
    to_block = jnp.where(core == 0, row, source)
    from_block = jnp.where(core == 0, source, row)
    upper = (from_block >= half).astype(jnp.int32)
    facts_v[0] = jnp.where(alive, to_block, blocks)
    facts_v[1] = from_block - upper * half + jnp.where(upper == core, 0, half)
    scalars = pltpu.make_async_copy(facts_v, facts_s, sem.at[0])
    scalars.start()
    scalars.wait()
    for n in range(len(qs)):
        for copy in copies[n]:
            copy.wait()
        for w in range(wide):
            t = n * wide + w
            terms = []
            for i in range(cap):
                terms.append(
                    jnp.dot(
                        tiles[t, i * side : (i + 1) * side, :],
                        feats[n * blocks + facts_s[1, t, i]],
                        preferred_element_type=F32,
                    )
                )
            for i in range(cap):
                to = facts_s[0, t, i]
                acc[to] = acc[to] + terms[i]
    for b in range(blocks):
        out_ref[b * side : (b + 1) * side, :] = acc[b].astype(BF)


def aggregate(scal, row_sets, col_sets, where, mine, other, blocks, side, cap):
    wide, narrow = len(row_sets), len(mine)
    qs = range(narrow)
    width = mine[0][0][0].shape[-1]
    arrays = []

    def place(array, index):
        for at, known in enumerate(arrays):
            if known is array:
                return at, index
        arrays.append(array)
        return len(arrays) - 1, index

    layout = dict(
        rows=[[place(a, None) for a in r] for r in row_sets],
        cols=[[place(a, None) for a in c] for c in col_sets],
        where=where,
        feats=[[[place(*p) for p in group] for group in (mine[q], other[q])] for q in qs],
        narrow=narrow,
    )
    layout["arrays"] = len(arrays)
    operands = list(arrays)
    count = len(qs) * wide
    shape = jax.ShapeDtypeStruct((blocks * side, width), BF)
    flops = 2 * count * cap * side * side * width
    return pl.pallas_call(
        functools.partial(aggregate_kernel, wide, cap, side, blocks, layout),
        out_shape=shape,
        in_specs=[pl.BlockSpec(memory_space=pltpu.SMEM)]
        + [pl.BlockSpec(memory_space=pl.ANY)] * len(operands),
        out_specs=pl.BlockSpec(memory_space=pltpu.VMEM),
        scratch_shapes=[
            pltpu.VMEM((count,) + row_sets[0][0].shape[-2:], BF),
            pltpu.VMEM((len(qs) * blocks, side, width), BF),
            pltpu.VMEM((blocks + 1, side, width), F32),
            pltpu.VMEM((2, count, side), jnp.int32),
            pltpu.SMEM((2, count, side), jnp.int32),
            pltpu.SemaphoreType.DMA((count,)),
            pltpu.SemaphoreType.DMA((len(qs) * CORES * 2,)),
            pltpu.SemaphoreType.DMA((1,)),
        ],
        compiler_params=pltpu.CompilerParams(vmem_limit_bytes=58 << 20),
        cost_estimate=pl.CostEstimate(
            flops=flops, bytes_accessed=count * cap * side * side * 15, transcendentals=0
        ),
    )(scal, *operands)


def joined(refs):
    return jnp.concatenate([r[...] for r in refs], axis=1)


def fill_weights(scal, refs, scratch, cols, across):
    self_ref, out_ref, in_ref = refs
    width = self_ref.shape[0]
    xs = width // cols
    core, chip = scal[0], scal[1]

    def put(at, value):
        if across:
            scratch[:, at : at + value.shape[1]] = value
        else:
            scratch[at : at + value.shape[0], :] = value

    put(0, self_ref[...])
    for d in range(CORES):
        for k in range(xs):
            rank = lax.rem(chip - k + xs, xs)
            out_w, in_w = out_ref[0], in_ref[0]
            for e in range(1, xs):
                out_w = jnp.where(rank == e, out_ref[e], out_w)
                in_w = jnp.where(rank == e, in_ref[e], in_w)
            use_out = (core == 0) == (d == 0)
            put(width + (d * xs + k) * cols, jnp.where(use_out, out_w, in_w))


def layer_kernel(parts, cols, scal, *refs):
    ins = refs[:parts]
    cotangent, *weights, hidden_ref, grad_ref, scratch = refs[parts:]

    @pl.when(pl.program_id(0) == 0)
    def _():
        fill_weights(scal, weights, scratch, cols, False)

    pre = jnp.dot(joined(ins), scratch[...], preferred_element_type=F32)
    sigma = 1.0 / (1.0 + jnp.exp(-pre))
    hidden_ref[...] = (pre * sigma).astype(BF)
    grad_ref[...] = (cotangent[...].astype(F32) * sigma * (1.0 + pre * (1.0 - sigma))).astype(BF)


def final_kernel(parts, cols, scal, *refs):
    ins = refs[:parts]
    *weights, out_ref, scratch = refs[parts:]

    @pl.when(pl.program_id(0) == 0)
    def _():
        fill_weights(scal, weights, scratch, cols, True)

    out_ref[...] = lax.dot_general(
        joined(ins), scratch[...], (((1,), (1,)), ((), ())), preferred_element_type=F32
    ).astype(BF)


def row_specs(arrays, step):
    return [pl.BlockSpec((step, a.shape[1]), lambda i: (i, 0)) for a in arrays]


def whole(a):
    return pl.BlockSpec(a.shape, lambda i: (0,) * a.ndim)


def over_rows_call(kernel, scal, ins, weights, cols, step, outs, across):
    rows, width = ins[0].shape
    xs = width // cols
    if across:
        split = [w.reshape(width, xs, cols).swapaxes(0, 1) for w in weights[1:]]
        scratch = (width, width * (1 + CORES))
    else:
        split = [w.reshape(xs, cols, width) for w in weights[1:]]
        scratch = (width * (1 + CORES), width)
    weights = [weights[0]] + split
    shape = jax.ShapeDtypeStruct((rows, width), BF)
    parts = 1 + CORES * xs
    result = pl.pallas_call(
        functools.partial(kernel, parts, cols),
        grid=(rows // step,),
        out_shape=(shape,) * outs,
        in_specs=[pl.BlockSpec(memory_space=pltpu.SMEM)]
        + row_specs(ins, step)
        + [whole(w) for w in weights],
        out_specs=tuple(row_specs([shape] * outs, step)),
        scratch_shapes=[pltpu.VMEM(scratch, BF)],
        compiler_params=pltpu.CompilerParams(vmem_limit_bytes=58 << 20),
    )(scal, *ins, *weights)
    return result if outs > 1 else result[0]


def body(node_feats, grad_out, tile_weight, tile_row, src_block, tile_count, w_self, w_out, w_in):
    wide, narrow = lax.axis_size("wide"), lax.axis_size("narrow")
    xs, zs, ys = dims(wide, narrow)
    slots = tile_row.shape[-1]
    cap = slots // narrow
    nodes, width = node_feats.shape
    side = tile_weight.shape[-1]
    blocks = nodes // side
    half = blocks // CORES
    cols = width // xs
    w_id, n_id = lax.axis_index("wide"), lax.axis_index("narrow")
    core, x_id = w_id % CORES, w_id // CORES
    z_id, y_id = n_id // ys, n_id % ys
    first = core == 0
    every = [(k, j) for k in range(zs) for j in range(ys)]

    def own_piece(a):
        piece = lax.dynamic_slice(a, (core * half * side, x_id * cols), (half * side, cols))
        return piece.reshape(half, side, cols)

    tiles = tile_weight.reshape(narrow, cap, side, side)
    live = jnp.arange(cap, dtype=jnp.int32)[None, :] < tile_count.reshape(narrow, 1)
    facts = jnp.stack(
        [
            tile_row.reshape(narrow, cap).astype(BF),
            src_block.reshape(narrow, cap).astype(BF),
            live.astype(BF),
        ],
        axis=1,
    )
    facts = jnp.pad(facts, ((0, 0), (0, META - 3), (0, side - cap)))

    def packed(t):
        return jnp.concatenate([t.reshape(narrow, cap * side, side), facts], axis=1)

    q = jnp.arange(narrow, dtype=jnp.int32)
    order = (z_id - q // ys) % zs * ys + (y_id - q % ys) % ys
    scal = jnp.concatenate([core.reshape(1), x_id.reshape(1), order]).astype(jnp.int32)

    def here(arrays):
        return [(a, None) for a in arrays]

    def swap(a, *ahead):
        return core_swap(after(a, *ahead), wide)

    def meet(a, bit):
        return lax.ppermute(a, "narrow", [(i, i ^ bit) for i in range(narrow)])

    def halve(a, bit, *ahead):
        upper = n_id // bit % 2
        halves = after(a, *ahead).reshape(2, -1, width)
        sent = lax.dynamic_index_in_dim(halves, 1 - upper, 0, keepdims=False)
        kept = lax.dynamic_index_in_dim(halves, upper, 0, keepdims=False)
        return kept + meet(sent, bit)

    def in_order(parts, at):
        count = len(parts)
        ahead = [parts[-i % count] for i in range(count)]
        return lax.dynamic_slice_in_dim(jnp.stack(ahead + ahead), count - at, count, 0)

    def along_x(a, *ahead):
        return [x_shift(after(a, *ahead), k, wide) for k in range(1, xs)]

    own = own_piece(node_feats)
    z1 = z_shift(own, 1, zs, ys)
    row_own = packed(after(tiles, own))
    row_x0 = along_x(row_own[: narrow // 2], own)
    col_by_owner = packed(after(tiles, row_own).swapaxes(2, 3))
    col_by_owner = col_by_owner.reshape(zs, ys, cap * side + META, side)
    toward = [
        lax.dynamic_index_in_dim(col_by_owner, (y_id + j) % ys, 1, keepdims=False)
        for j in range(ys)
    ]
    moved = [y_shift(toward[j], j, zs, ys) for j in range(1, ys)]
    one = [z1] + moved + row_x0
    col_by_z = jnp.stack([toward[0]] + [after(m, *one) for m in moved], axis=1)

    def col_part(k, *ahead):
        part = lax.dynamic_index_in_dim(col_by_z, (z_id + k) % zs, 0, keepdims=False)
        return after(part, *ahead)

    s1 = z_shift(col_part(1, *one), 1, zs, ys)
    s3 = z_shift(col_part(3, *one), 3, zs, ys)
    y0 = y_shift(after(own, *one), 1, zs, ys)
    row_x1 = along_x(row_own[narrow // 2 :], *one)
    row_swap = swap(row_own, *one)
    two = [s1, s3, y0, row_swap] + row_x1
    z2 = z_shift(after(z1, *two), 1, zs, ys)
    y1 = y_shift(after(z1, *two), 1, zs, ys)
    near = jnp.concatenate([col_part(0, *one), s1], axis=0)
    near_x = along_x(near, *two)
    own_swap, z1_swap = swap(own, *two), swap(z1, *two)
    three = [z2, y1, own_swap, z1_swap] + near_x
    z3 = z_shift(after(z2, *three), 1, zs, ys)
    y2 = y_shift(after(z2, *three), 1, zs, ys)
    s3_x = along_x(s3, *three)
    y0_swap = swap(y0, *three)
    row_x0_swap = [swap(a, *three) for a in row_x0]
    four = [z3, y2, y0_swap] + s3_x + row_x0_swap
    y3 = y_shift(after(z3, *four), 1, zs, ys)
    s2 = z_shift(col_part(2, *four), 2, zs, ys)
    z2_swap, y1_swap = swap(z2, *four), swap(y1, *four)
    row_x1_swap = [swap(a, *four) for a in row_x1]
    five = [y3, s2, z2_swap, y1_swap] + row_x1_swap
    s2_x = along_x(s2, *five)
    z3_swap, y2_swap = swap(z3, *five), swap(y2, *five)
    near_swap = [swap(a, *five) for a in [near] + near_x]
    six = [z3_swap, y2_swap] + s2_x + near_swap
    y3_swap = swap(y3, *six)
    s3_swap = [swap(a, *six) for a in [s3] + s3_x]
    s2_swap = [swap(a, *six) for a in [s2] + s2_x]

    row_sets = [[row_own, row_own]] + [list(p) for p in zip(row_x0, row_x1)]
    row_sets += [[row_swap, row_swap]] + [list(p) for p in zip(row_x0_swap, row_x1_swap)]
    col_sets = [list(p) for p in zip([near] + near_x, [s3] + s3_x, [s2] + s2_x)]
    col_sets += [list(p) for p in zip(near_swap, s3_swap, s2_swap)]
    where = {}
    for i, (k, j) in enumerate(every):
        where[i] = {0: (0, i), 1: (0, i), 2: (2, j), 3: (1, j)}[k]

    def spread(pieces, swaps, *ahead):
        for kj in every:
            if kj not in pieces:
                pieces[kj] = y_shift(pieces[kj[0], kj[1] - 1], 1, zs, ys)
            if kj not in swaps:
                swaps[kj] = core_swap(pieces[kj], wide)
        own = aggregate(
            after(scal, *ahead) if ahead else scal, row_sets, col_sets, where, [here([pieces[kj]]) for kj in every],
            [here([swaps[kj]]) for kj in every], blocks, side, cap,
        )
        return own, [own] + along_x(own), core_swap(own, wide)

    names = [(0, 0), (1, 0), (2, 0), (3, 0), (0, 1), (1, 1), (2, 1), (3, 1)]
    agg, aggs, agg_swap = spread(
        dict(zip(names, [own, z1, z2, z3, y0, y1, y2, y3])),
        dict(zip(names, [own_swap, z1_swap, z2_swap, z3_swap, y0_swap, y1_swap, y2_swap, y3_swap])),
    )
    aggs += [agg_swap] + [swap(a) for a in aggs[1:]]
    hidden, grad_pre = over_rows_call(
        layer_kernel, scal, [node_feats] + aggs + [grad_out], [w_self, w_out, w_in], cols,
        nodes // 2, 2, False,
    )

    own = own_piece(grad_pre)
    z1 = z_shift(own, 1, zs, ys)
    y0 = y_shift(own, 1, zs, ys)
    share = width // wide
    feat_part = lax.dynamic_slice(node_feats, (0, w_id * share), (nodes, share))
    grad_part = lax.dot_general(
        jnp.concatenate([agg, feat_part], axis=1),
        after(grad_pre, own),
        (((0,), (0,)), ((), ())),
        preferred_element_type=F32,
    )
    one = [z1, y0]
    z2 = z_shift(after(z1, *one), 1, zs, ys)
    y1 = y_shift(after(z1, *one), 1, zs, ys)
    grad_some = halve(grad_part, 1, *one)
    own_swap, z1_swap = swap(own, *one), swap(z1, *one)
    two = [z2, y1, own_swap, z1_swap, grad_some]
    z3 = z_shift(after(z2, *two), 1, zs, ys)
    y2 = y_shift(after(z2, *two), 1, zs, ys)
    y0_swap, z2_swap = swap(y0, *two), swap(z2, *two)
    for bit in range(2, ys, 2):
        grad_some = halve(grad_some, bit, *two)
    grad_some = halve(grad_some, 2 * ys, *two)
    three = [z3, y2, y0_swap, z2_swap, grad_some]
    quarter = half // 2
    y3 = y_shift(after(z3, *three)[:quarter], 1, zs, ys)
    y3_rest = z_shift(after(y2, *three)[quarter:], 1, zs, ys)
    grad_some = halve(grad_some, ys, *three)
    y1_swap, z3_swap = swap(y1, *three), swap(z3, *three)
    four = [y3, y3_rest, y1_swap, z3_swap, grad_some]
    y3 = jnp.concatenate([y3, y3_rest], axis=0)
    y2_swap, y3_swap = swap(y2, *four), swap(y3, *four)
    grad_some = after(grad_some, *four)
    chips = [grad_some] + along_x(grad_some)
    shared = in_order(chips, x_id)
    _, backs, back_swap = spread(
        dict(zip(names, [own, z1, z2, z3, y0, y1, y2, y3])),
        dict(zip(names, [own_swap, z1_swap, z2_swap, z3_swap, y0_swap, y1_swap, y2_swap, y3_swap])),
        shared,
    )
    shared = after(shared, back_swap)
    stack = in_order([shared] + [z_shift(shared, k, zs, ys) for k in range(1, zs)], z_id)
    stack = stack.swapaxes(0, 1).reshape(xs, -1, width)
    stack = in_order([stack] + [y_shift(stack, j, zs, ys) for j in range(1, ys)], y_id)
    stack = stack.swapaxes(0, 1).reshape(xs, -1, width)
    stack = in_order([stack, core_swap(stack, wide)], core)
    agg_grads = stack[:, :, :cols].reshape(CORES, width, width)
    grad_ws = stack[:, :, cols:].swapaxes(0, 1).reshape(width, width)

    backs += [back_swap] + [swap(a) for a in backs[1:]]
    grad_feats = over_rows_call(
        final_kernel, scal, [grad_pre] + backs, [w_self, w_in, w_out], cols, nodes // 2, 1, True
    )
    return (hidden, grad_feats, grad_ws, agg_grads[0], agg_grads[1])


def solution(mesh):
    return jax.shard_map(
        body,
        mesh=mesh,
        in_specs=(
            P("narrow", None),
            P("narrow", None),
            P("wide", "narrow", None, None, None),
            P("wide", "narrow", None),
            P("wide", "narrow", None),
            P("wide", "narrow", None),
            P(),
            P(),
            P(),
        ),
        out_specs=(P("narrow", None), P("narrow", None), P(), P(), P()),
        check_vma=False,
    )
```

```python
import functools

import jax
import jax.numpy as jnp
from jax import lax
from jax.experimental import pallas as pl
from jax.experimental.pallas import tpu as pltpu
from jax.sharding import PartitionSpec as P

BF = jnp.bfloat16
F32 = jnp.float32
META = 16
CORES = 2


def dims(wide, narrow):
    z = 4 if narrow % 4 == 0 else 1
    return wide // CORES, z, narrow // z


def x_shift(a, k, wide):
    return lax.ppermute(a, "wide", [(i, (i + CORES * k) % wide) for i in range(wide)])


def core_swap(a, wide):
    return lax.ppermute(a, "wide", [(i, i ^ 1) for i in range(wide)])


def z_shift(a, k, zs, ys):
    return lax.ppermute(
        a, "narrow", [(z * ys + y, (z + k) % zs * ys + y) for z in range(zs) for y in range(ys)]
    )


def y_shift(a, k, zs, ys):
    return lax.ppermute(
        a, "narrow", [(z * ys + y, z * ys + (y + k) % ys) for z in range(zs) for y in range(ys)]
    )


def after(a, *others):
    return lax.optimization_barrier((a,) + others)[0]


def aggregate_kernel(wide, cap, side, blocks, layout, scal, *refs):
    qs = range(layout["narrow"])
    half = blocks // CORES
    refs = list(refs)
    arrays = [refs.pop(0) for _ in range(layout["arrays"])]
    row_sets, col_sets = layout["rows"], layout["cols"]
    out_ref, tiles, feats, acc, facts_v, facts_s, tile_sem, feat_sem, sem = refs

    def take(place):
        at, index = place
        return arrays[at] if index is None else arrays[at].at[index]

    def col_copy(n, w):
        part, start = layout["where"][n]
        return pltpu.make_async_copy(
            take(col_sets[w][part]).at[start],
            tiles.at[n * wide + w],
            tile_sem.at[n * wide + w],
        )

    @pl.when(scal[0] == 0)
    def _():
        for n in range(len(qs)):
            owner = scal[2 + n]
            for w in range(wide):
                low, high = (take(r) for r in row_sets[w])
                into, done = tiles.at[n * wide + w], tile_sem.at[n * wide + w]
                if row_sets[w][0] == row_sets[w][1]:
                    pltpu.make_async_copy(low.at[owner], into, done).start()
                else:
                    split = len(qs) // 2

                    @pl.when(owner < split)
                    def _():
                        pltpu.make_async_copy(low.at[owner], into, done).start()

                    @pl.when(owner >= split)
                    def _():
                        pltpu.make_async_copy(high.at[owner - split], into, done).start()

    @pl.when(scal[0] != 0)
    def _():
        for n in range(len(qs)):
            for w in range(wide):
                col_copy(n, w).start()

    copies = []
    for n in range(len(qs)):
        here = []
        for h, group in enumerate(layout["feats"][n]):
            size = half // len(group)
            for e, place in enumerate(group):
                source = take(place)
                copy = pltpu.make_async_copy(
                    source,
                    feats.at[pl.ds(n * blocks + h * half + e * size, size)],
                    feat_sem.at[(n * CORES + h) * 2 + e],
                )
                copy.start()
                here.append(copy)
        copies.append(here)
    acc[...] = jnp.zeros_like(acc)
    for n in range(len(qs)):
        for w in range(wide):
            col_copy(n, w).wait()
    core = scal[0]
    facts = tiles[:, cap * side : cap * side + META, :].astype(F32)
    row = facts[:, 0, :].astype(jnp.int32)
    source = facts[:, 1, :].astype(jnp.int32)
    alive = facts[:, 2, :] > 0.5
    to_block = jnp.where(core == 0, row, source)
    from_block = jnp.where(core == 0, source, row)
    upper = (from_block >= half).astype(jnp.int32)
    facts_v[0] = jnp.where(alive, to_block, blocks)
    facts_v[1] = from_block - upper * half + jnp.where(upper == core, 0, half)
    scalars = pltpu.make_async_copy(facts_v, facts_s, sem.at[0])
    scalars.start()
    scalars.wait()
    for n in range(len(qs)):
        for copy in copies[n]:
            copy.wait()
        for w in range(wide):
            t = n * wide + w
            terms = []
            for i in range(cap):
                terms.append(
                    jnp.dot(
                        tiles[t, i * side : (i + 1) * side, :],
                        feats[n * blocks + facts_s[1, t, i]],
                        preferred_element_type=F32,
                    )
                )
            for i in range(cap):
                to = facts_s[0, t, i]
                acc[to] = acc[to] + terms[i]
    for b in range(blocks):
        out_ref[b * side : (b + 1) * side, :] = acc[b].astype(BF)


def aggregate(scal, row_sets, col_sets, where, mine, other, blocks, side, cap):
    wide, narrow = len(row_sets), len(mine)
    qs = range(narrow)
    width = mine[0][0][0].shape[-1]
    arrays = []

    def place(array, index):
        for at, known in enumerate(arrays):
            if known is array:
                return at, index
        arrays.append(array)
        return len(arrays) - 1, index

    layout = dict(
        rows=[[place(a, None) for a in r] for r in row_sets],
        cols=[[place(a, None) for a in c] for c in col_sets],
        where=where,
        feats=[[[place(*p) for p in group] for group in (mine[q], other[q])] for q in qs],
        narrow=narrow,
    )
    layout["arrays"] = len(arrays)
    operands = list(arrays)
    count = len(qs) * wide
    shape = jax.ShapeDtypeStruct((blocks * side, width), BF)
    flops = 2 * count * cap * side * side * width
    return pl.pallas_call(
        functools.partial(aggregate_kernel, wide, cap, side, blocks, layout),
        out_shape=shape,
        in_specs=[pl.BlockSpec(memory_space=pltpu.SMEM)]
        + [pl.BlockSpec(memory_space=pl.ANY)] * len(operands),
        out_specs=pl.BlockSpec(memory_space=pltpu.VMEM),
        scratch_shapes=[
            pltpu.VMEM((count,) + row_sets[0][0].shape[-2:], BF),
            pltpu.VMEM((len(qs) * blocks, side, width), BF),
            pltpu.VMEM((blocks + 1, side, width), F32),
            pltpu.VMEM((2, count, side), jnp.int32),
            pltpu.SMEM((2, count, side), jnp.int32),
            pltpu.SemaphoreType.DMA((count,)),
            pltpu.SemaphoreType.DMA((len(qs) * CORES * 2,)),
            pltpu.SemaphoreType.DMA((1,)),
        ],
        compiler_params=pltpu.CompilerParams(vmem_limit_bytes=58 << 20),
        cost_estimate=pl.CostEstimate(
            flops=flops, bytes_accessed=count * cap * side * side * 15, transcendentals=0
        ),
    )(scal, *operands)


def joined(refs):
    return jnp.concatenate([r[...] for r in refs], axis=1)


def fill_weights(scal, refs, scratch, cols, across):
    self_ref, out_ref, in_ref = refs
    width = self_ref.shape[0]
    xs = width // cols
    core, chip = scal[0], scal[1]

    def put(at, value):
        if across:
            scratch[:, at : at + value.shape[1]] = value
        else:
            scratch[at : at + value.shape[0], :] = value

    put(0, self_ref[...])
    for d in range(CORES):
        for k in range(xs):
            rank = lax.rem(chip - k + xs, xs)
            out_w, in_w = out_ref[0], in_ref[0]
            for e in range(1, xs):
                out_w = jnp.where(rank == e, out_ref[e], out_w)
                in_w = jnp.where(rank == e, in_ref[e], in_w)
            use_out = (core == 0) == (d == 0)
            put(width + (d * xs + k) * cols, jnp.where(use_out, out_w, in_w))


def layer_kernel(parts, cols, scal, *refs):
    ins = refs[:parts]
    cotangent, *weights, hidden_ref, grad_ref, piece_ref, scratch = refs[parts:]

    @pl.when(pl.program_id(0) == 0)
    def _():
        fill_weights(scal, weights, scratch, cols, False)

    pre = jnp.dot(joined(ins), scratch[...], preferred_element_type=F32)
    sigma = 1.0 / (1.0 + jnp.exp(-pre))
    hidden_ref[...] = (pre * sigma).astype(BF)
    slope = (cotangent[...].astype(F32) * sigma * (1.0 + pre * (1.0 - sigma))).astype(BF)
    grad_ref[...] = slope

    @pl.when(pl.program_id(0) == scal[0])
    def _():
        piece = slope[:, :cols]
        for e in range(1, slope.shape[1] // cols):
            piece = jnp.where(scal[1] == e, slope[:, e * cols : (e + 1) * cols], piece)
        piece_ref[...] = piece


def final_kernel(parts, cols, scal, *refs):
    ins = refs[:parts]
    *weights, out_ref, scratch = refs[parts:]

    @pl.when(pl.program_id(0) == 0)
    def _():
        fill_weights(scal, weights, scratch, cols, True)

    out_ref[...] = lax.dot_general(
        joined(ins), scratch[...], (((1,), (1,)), ((), ())), preferred_element_type=F32
    ).astype(BF)


def row_specs(arrays, step):
    return [pl.BlockSpec((step, a.shape[1]), lambda i: (i, 0)) for a in arrays]


def whole(a):
    return pl.BlockSpec(a.shape, lambda i: (0,) * a.ndim)


def over_rows_call(kernel, scal, ins, weights, cols, step, outs, across):
    rows, width = ins[0].shape
    xs = width // cols
    if across:
        split = [w.reshape(width, xs, cols).swapaxes(0, 1) for w in weights[1:]]
        scratch = (width, width * (1 + CORES))
    else:
        split = [w.reshape(xs, cols, width) for w in weights[1:]]
        scratch = (width * (1 + CORES), width)
    weights = [weights[0]] + split
    shape = jax.ShapeDtypeStruct((rows, width), BF)
    parts = 1 + CORES * xs
    extra = (jax.ShapeDtypeStruct((step, cols), BF),) if outs > 1 else ()
    result = pl.pallas_call(
        functools.partial(kernel, parts, cols),
        grid=(rows // step,),
        out_shape=(shape,) * outs + extra,
        in_specs=[pl.BlockSpec(memory_space=pltpu.SMEM)]
        + row_specs(ins, step)
        + [whole(w) for w in weights],
        out_specs=tuple(row_specs([shape] * outs, step)) + tuple(whole(e) for e in extra),
        scratch_shapes=[pltpu.VMEM(scratch, BF)],
        compiler_params=pltpu.CompilerParams(vmem_limit_bytes=58 << 20),
    )(scal, *ins, *weights)
    return result if outs > 1 else result[0]


def body(node_feats, grad_out, tile_weight, tile_row, src_block, tile_count, w_self, w_out, w_in):
    wide, narrow = lax.axis_size("wide"), lax.axis_size("narrow")
    xs, zs, ys = dims(wide, narrow)
    slots = tile_row.shape[-1]
    cap = slots // narrow
    nodes, width = node_feats.shape
    side = tile_weight.shape[-1]
    blocks = nodes // side
    half = blocks // CORES
    cols = width // xs
    w_id, n_id = lax.axis_index("wide"), lax.axis_index("narrow")
    core, x_id = w_id % CORES, w_id // CORES
    z_id, y_id = n_id // ys, n_id % ys
    first = core == 0
    every = [(k, j) for k in range(zs) for j in range(ys)]

    def own_piece(a):
        piece = lax.dynamic_slice(a, (core * half * side, x_id * cols), (half * side, cols))
        return piece.reshape(half, side, cols)

    tiles = tile_weight.reshape(narrow, cap, side, side)
    live = jnp.arange(cap, dtype=jnp.int32)[None, :] < tile_count.reshape(narrow, 1)
    facts = jnp.stack(
        [
            tile_row.reshape(narrow, cap).astype(BF),
            src_block.reshape(narrow, cap).astype(BF),
            live.astype(BF),
        ],
        axis=1,
    )
    facts = jnp.pad(facts, ((0, 0), (0, META - 3), (0, side - cap)))

    def packed(t):
        return jnp.concatenate([t.reshape(narrow, cap * side, side), facts], axis=1)

    q = jnp.arange(narrow, dtype=jnp.int32)
    order = (z_id - q // ys) % zs * ys + (y_id - q % ys) % ys
    scal = jnp.concatenate([core.reshape(1), x_id.reshape(1), order]).astype(jnp.int32)

    def here(arrays):
        return [(a, None) for a in arrays]

    def swap(a, *ahead):
        return core_swap(after(a, *ahead), wide)

    def meet(a, bit):
        return lax.ppermute(a, "narrow", [(i, i ^ bit) for i in range(narrow)])

    def halve(a, bit, *ahead):
        upper = n_id // bit % 2
        halves = after(a, *ahead).reshape(2, -1, width)
        sent = lax.dynamic_index_in_dim(halves, 1 - upper, 0, keepdims=False)
        kept = lax.dynamic_index_in_dim(halves, upper, 0, keepdims=False)
        return kept + meet(sent, bit)

    def in_order(parts, at):
        count = len(parts)
        ahead = [parts[-i % count] for i in range(count)]
        return lax.dynamic_slice_in_dim(jnp.stack(ahead + ahead), count - at, count, 0)

    def along_x(a, *ahead):
        return [x_shift(after(a, *ahead), k, wide) for k in range(1, xs)]

    own = own_piece(node_feats)
    z1 = z_shift(own, 1, zs, ys)
    row_own = packed(after(tiles, own))
    row_x0 = along_x(row_own[: narrow // 2], own)
    col_by_owner = packed(after(tiles, row_own).swapaxes(2, 3))
    col_by_owner = col_by_owner.reshape(zs, ys, cap * side + META, side)
    toward = [
        lax.dynamic_index_in_dim(col_by_owner, (y_id + j) % ys, 1, keepdims=False)
        for j in range(ys)
    ]
    moved = [y_shift(toward[j], j, zs, ys) for j in range(1, ys)]
    one = [z1] + moved + row_x0
    col_by_z = jnp.stack([toward[0]] + [after(m, *one) for m in moved], axis=1)

    def col_part(k, *ahead):
        part = lax.dynamic_index_in_dim(col_by_z, (z_id + k) % zs, 0, keepdims=False)
        return after(part, *ahead)

    s1 = z_shift(col_part(1, *one), 1, zs, ys)
    s3 = z_shift(col_part(3, *one), 3, zs, ys)
    y0 = y_shift(after(own, *one), 1, zs, ys)
    row_x1 = along_x(row_own[narrow // 2 :], *one)
    row_swap = swap(row_own, *one)
    two = [s1, s3, y0, row_swap] + row_x1
    z2 = z_shift(after(z1, *two), 1, zs, ys)
    y1 = y_shift(after(z1, *two), 1, zs, ys)
    near = jnp.concatenate([col_part(0, *one), s1], axis=0)
    near_x = along_x(near, *two)
    own_swap, z1_swap = swap(own, *two), swap(z1, *two)
    three = [z2, y1, own_swap, z1_swap] + near_x
    z3 = z_shift(after(z2, *three), 1, zs, ys)
    y2 = y_shift(after(z2, *three), 1, zs, ys)
    s3_x = along_x(s3, *three)
    y0_swap = swap(y0, *three)
    row_x0_swap = [swap(a, *three) for a in row_x0]
    four = [z3, y2, y0_swap] + s3_x + row_x0_swap
    y3 = y_shift(after(z3, *four), 1, zs, ys)
    s2 = z_shift(col_part(2, *four), 2, zs, ys)
    z2_swap, y1_swap = swap(z2, *four), swap(y1, *four)
    row_x1_swap = [swap(a, *four) for a in row_x1]
    five = [y3, s2, z2_swap, y1_swap] + row_x1_swap
    s2_x = along_x(s2, *five)
    z3_swap, y2_swap = swap(z3, *five), swap(y2, *five)
    near_swap = [swap(a, *five) for a in [near] + near_x]
    six = [z3_swap, y2_swap] + s2_x + near_swap
    y3_swap = swap(y3, *six)
    s3_swap = [swap(a, *six) for a in [s3] + s3_x]
    s2_swap = [swap(a, *six) for a in [s2] + s2_x]

    row_sets = [[row_own, row_own]] + [list(p) for p in zip(row_x0, row_x1)]
    row_sets += [[row_swap, row_swap]] + [list(p) for p in zip(row_x0_swap, row_x1_swap)]
    col_sets = [list(p) for p in zip([near] + near_x, [s3] + s3_x, [s2] + s2_x)]
    col_sets += [list(p) for p in zip(near_swap, s3_swap, s2_swap)]
    where = {}
    for i, (k, j) in enumerate(every):
        where[i] = {0: (0, i), 1: (0, i), 2: (2, j), 3: (1, j)}[k]

    def spread(pieces, swaps, *ahead):
        for kj in every:
            if kj not in pieces:
                pieces[kj] = y_shift(pieces[kj[0], kj[1] - 1], 1, zs, ys)
            if kj not in swaps:
                swaps[kj] = core_swap(pieces[kj], wide)
        own = aggregate(
            after(scal, *ahead) if ahead else scal, row_sets, col_sets, where, [here([pieces[kj]]) for kj in every],
            [here([swaps[kj]]) for kj in every], blocks, side, cap,
        )
        return own, [own] + along_x(own), core_swap(own, wide)

    names = [(0, 0), (1, 0), (2, 0), (3, 0), (0, 1), (1, 1), (2, 1), (3, 1)]
    agg, aggs, agg_swap = spread(
        dict(zip(names, [own, z1, z2, z3, y0, y1, y2, y3])),
        dict(zip(names, [own_swap, z1_swap, z2_swap, z3_swap, y0_swap, y1_swap, y2_swap, y3_swap])),
    )
    aggs += [agg_swap] + [swap(a) for a in aggs[1:]]
    hidden, grad_pre, own = over_rows_call(
        layer_kernel, scal, [node_feats] + aggs + [grad_out], [w_self, w_out, w_in], cols,
        nodes // CORES, 2, False,
    )

    own = own.reshape(half, side, cols)
    z1 = z_shift(own, 1, zs, ys)
    y0 = y_shift(own, 1, zs, ys)
    share = width // wide
    feat_part = lax.dynamic_slice(node_feats, (0, w_id * share), (nodes, share))
    grad_part = lax.dot_general(
        jnp.concatenate([agg, feat_part], axis=1),
        after(grad_pre, own),
        (((0,), (0,)), ((), ())),
        preferred_element_type=F32,
    )
    one = [z1, y0]
    z2 = z_shift(after(z1, *one), 1, zs, ys)
    y1 = y_shift(after(z1, *one), 1, zs, ys)
    grad_some = halve(grad_part, 1, *one)
    own_swap, z1_swap = swap(own, *one), swap(z1, *one)
    two = [z2, y1, own_swap, z1_swap, grad_some]
    z3 = z_shift(after(z2, *two), 1, zs, ys)
    y2 = y_shift(after(z2, *two), 1, zs, ys)
    y0_swap, z2_swap = swap(y0, *two), swap(z2, *two)
    for bit in range(2, ys, 2):
        grad_some = halve(grad_some, bit, *two)
    grad_some = halve(grad_some, 2 * ys, *two)
    three = [z3, y2, y0_swap, z2_swap, grad_some]
    quarter = half // 2
    y3 = y_shift(after(z3, *three)[:quarter], 1, zs, ys)
    y3_rest = z_shift(after(y2, *three)[quarter:], 1, zs, ys)
    grad_some = halve(grad_some, ys, *three)
    y1_swap, z3_swap = swap(y1, *three), swap(z3, *three)
    four = [y3, y3_rest, y1_swap, z3_swap, grad_some]
    y3 = jnp.concatenate([y3, y3_rest], axis=0)
    y2_swap, y3_swap = swap(y2, *four), swap(y3, *four)
    grad_some = after(grad_some, *four)
    chips = [grad_some] + along_x(grad_some)
    shared = in_order(chips, x_id)
    _, backs, back_swap = spread(
        dict(zip(names, [own, z1, z2, z3, y0, y1, y2, y3])),
        dict(zip(names, [own_swap, z1_swap, z2_swap, z3_swap, y0_swap, y1_swap, y2_swap, y3_swap])),
        shared,
    )
    shared = after(shared, back_swap)
    stack = in_order([shared] + [z_shift(shared, k, zs, ys) for k in range(1, zs)], z_id)
    stack = stack.swapaxes(0, 1).reshape(xs, -1, width)
    stack = in_order([stack] + [y_shift(stack, j, zs, ys) for j in range(1, ys)], y_id)
    stack = stack.swapaxes(0, 1).reshape(xs, -1, width)
    stack = in_order([stack, core_swap(stack, wide)], core)
    agg_grads = stack[:, :, :cols].reshape(CORES, width, width)
    grad_ws = stack[:, :, cols:].swapaxes(0, 1).reshape(width, width)

    backs += [back_swap] + [swap(a, stack) for a in backs[1:]]
    grad_feats = over_rows_call(
        final_kernel, scal, [grad_pre] + backs, [w_self, w_in, w_out], cols, nodes // CORES, 1, True
    )
    return (hidden, grad_feats, grad_ws, agg_grads[0], agg_grads[1])


def solution(mesh):
    return jax.shard_map(
        body,
        mesh=mesh,
        in_specs=(
            P("narrow", None),
            P("narrow", None),
            P("wide", "narrow", None, None, None),
            P("wide", "narrow", None),
            P("wide", "narrow", None),
            P("wide", "narrow", None),
            P(),
            P(),
            P(),
        ),
        out_specs=(P("narrow", None), P("narrow", None), P(), P(), P()),
        check_vma=False,
    )
```
